32 devices in a mesh: groups: 2 (over y), dom: 4 (over z), sub: 2 (over x), rep: 2 (over core).
Axes of the slice: x: 2, y: 2, z: 4, core: 2. Of those that a mesh axis runs over, the one named last changes fastest.
Arguments:
- state_pre: bfloat16 [65536, 256], P(('groups', 'dom', 'sub'), 'rep'), parts along dimension 0, may hold values from -4 to 4
- loss_grad: bfloat16 [65536, 256], P(('groups', 'dom', 'sub'), 'rep'), parts along dimension 0, may hold values from -6 to 6
- weight: bfloat16 [256, 256], P('rep'), may hold values from -0.375 to 0.375
- live_counts: int32 [16], P(('groups', 'dom', 'sub')), parts along dimension 0, may hold values from 1 to 4096, 24576 in all
- partners: int32 [16, 96, 1], P(('groups', 'dom', 'sub')), parts along dimension 0, may hold values from 0 to 7; in each aligned block of 96 rows (0 to 95, 96 to 191, ..., all dimensions but the last counted through in order) at most 16 rows name the same one
- row_tiles: int32 [16, 96], P(('groups', 'dom', 'sub')), parts along dimension 0, may hold values from 0 to 31
- col_tiles: int32 [16, 96], P(('groups', 'dom', 'sub')), parts along dimension 0, may hold values from 0 to 31
- block_tiles: bfloat16 [16, 96, 128, 128], P(('groups', 'dom', 'sub')), parts along dimension 0, may hold values from -0.15625 to 0.15625
Outputs:
- adjoint: bfloat16 [65536, 256], P(('groups', 'dom', 'sub'), 'rep'), parts along dimension 0
- weight_grad: float32 [512, 256], P(('groups', 'rep')), parts along dimension 0
The draws below stay inside these ranges and needn't reach their ends.
There are 2 independent parts, one for each index of `groups`. The reference program is written for one: setup_inputs(seed, part) draws one part's arguments, and reference() takes and returns one part's arrays. A program takes and returns all parts, laid end to end along the dimension named above; an argument that names none is the same for every part. Nothing has to cross between parts.
Inputs may be any that keep to these rules, and one draw needn't show every extreme that they name: `partners`: among one partition's 96 blocks no partition is named more than 16 times, a bound that some block reaches. `live_counts`: live nodes are the first slots of a partition; the counts sum to 24576 and the largest is 4096.
All inputs are finite; a program needn't handle non-finite values. No bound on the sum of `live_counts` on one device may be relied on, other than what follows from the above.
Results may differ from the reference program's by a relative error of at most 0.0058.
Values may be sent and summed in bfloat16 or wider, within the bound.
A program may use at most 128 MiB of HBM per device.

```python
import math
import jax
import jax.numpy as jnp
import numpy as np
from jax import lax

D = 256
CAP = 4096
BR = 128
BLOCKS = 96
ITERS = 3
PARTITIONS = 8
MOST = 16
NODES = 32768
LIVE_TOTAL = 24576


def with_ends(values, rng, low, top_value):
    place = [jax.random.randint(jax.random.fold_in(rng, axis), (), 0, length) for axis, length in enumerate(values.shape)]
    longest = values.shape.index(max(values.shape))
    beside = place[:longest] + [(place[longest] + 1) % values.shape[longest]] + place[longest + 1:]
    return values.at[tuple(place)].set(low).at[tuple(beside)].set(top_value)


def level_of(stream_key, shape, split, least, top_value):
    loudness, own = 1.0, jax.random.fold_in(stream_key, 6)
    for dim, shards_of in split:
        steps = jnp.exp(jax.random.uniform(jax.random.fold_in(own, dim), (shards_of,), jnp.float32, least / len(split), top_value / len(split)))
        loudness = loudness * jnp.repeat(steps, shape[dim] // shards_of).reshape([-1 if axis == dim else 1 for axis in range(len(shape))])
    return loudness


def profile(count, total, limit, slope):
    portions = [(1 << 20) // math.isqrt(rank ** slope) + 1 for rank in range(2, count + 1)]
    rest, holding = total - limit - (count - 1), [1] * (count - 1)
    while rest > 0:
        free = [i for i in range(count - 1) if holding[i] < limit]
        whole, budget = sum([portions[i] for i in free]), rest
        for i in free:
            more = min(limit - holding[i], max(1, budget * portions[i] // whole), rest)
            holding[i] = holding[i] + more
            rest = rest - more
    return np.array([limit] + holding)


def uneven_parts(stream_key, count, total, reach, skew):
    if count == 2:
        one = jax.random.randint(stream_key, (), max(1, total - reach), min(reach, total - 1) + 1)
        return jnp.stack([one, total - one])
    sizes = jnp.asarray(profile(count, total, reach, skew), jnp.int32)
    couples = (count - 1) // 2
    donor, taker = sizes[1:1 + 2 * couples:2], sizes[2:2 + 2 * couples:2]
    room = jnp.minimum(donor - 1, reach - taker)
    passed = jax.random.randint(jax.random.fold_in(stream_key, 1), (couples,), 0, 1 << 20) % (room + 1)
    sizes = sizes.at[1:1 + 2 * couples:2].set(donor - passed).at[2:2 + 2 * couples:2].set(taker + passed)
    return sizes[jax.random.permutation(jax.random.fold_in(stream_key, 2), count)]


def deal_out(own_key, own, number, rows, count, top, most, slope):
    ranking = jax.random.permutation(own_key, count)
    heavy_load, usual = portions_of(count, rows * top, most, slope, True), portions_of(count, rows * top, most, slope, False)
    places = jnp.arange(count)

    def named(sizes, turn):
        used = int((sizes > 0).sum())
        fixed = max(1, used // 4)
        moved = fixed + (places - fixed + turn * (used - fixed)) % max(1, count - fixed)
        return jnp.zeros((count,), jnp.int32).at[ranking[jnp.where(places < fixed, places, moved)]].set(jnp.asarray(sizes, jnp.int32))

    sizes = jnp.where(number % 4 == 0, named(heavy_load, number // 4), named(usual, number - number // 4 - 1))
    mixed = jax.random.permutation(jax.random.fold_in(own, 3), count)
    giver, receiver = mixed[0:count // 2 * 2:2], mixed[1:count // 2 * 2:2]
    room = jnp.minimum(sizes[giver] - 1, most - sizes[receiver]) // 2
    room = jnp.where((giver == ranking[0]) | (receiver == ranking[0]) | (sizes[receiver] == 0), 0, jnp.maximum(room, 0))
    moved = jax.random.randint(jax.random.fold_in(own, 4), (count // 2,), 0, 1 << 20) % (room + 1)
    sizes = sizes.at[giver].add(-moved).at[receiver].add(moved)
    members = jnp.searchsorted(jnp.cumsum(sizes), jnp.arange(rows * top), side="right").astype(jnp.int32)
    table = members.reshape(top, rows).T
    table = table[jax.random.permutation(jax.random.fold_in(own, 1), rows)]
    turn = jax.random.randint(jax.random.fold_in(own, 2), (rows, 1), 0, top)
    return jnp.take_along_axis(table, (jnp.arange(top)[None, :] + turn) % top, axis=1)


def portions_of(number_of, total, reach, skew, full):
    loads = [(1 << 20) // math.isqrt(standing ** skew) + 1 for standing in range(1, number_of + 1)]
    largest = reach if full else min(reach, max(-(-total // number_of), total * loads[0] // sum(loads)))
    least = 1 if total - largest >= number_of - 1 else 0
    holding, spare = [largest] + [least] * (number_of - 1), total - largest - least * (number_of - 1)
    while spare > 0:
        movable = [i for i in range(1, number_of) if holding[i] < largest] or [i for i in range(1, number_of) if holding[i] < reach]
        pool, remaining = sum([loads[i] for i in movable]), spare
        for i in movable:
            addition = min(reach - holding[i], max(1, remaining * loads[i] // pool), spare)
            holding[i] = holding[i] + addition
            spare = spare - addition
    return np.array(holding)


def noise(key, extent, scale, reach, shards=(), kind=jnp.bfloat16):
    drawn = jax.random.normal(key, extent, jnp.float32) * scale
    if len(shards) > 0:
        drawn = level_of(key, extent, shards, -0.22, 0.18) * drawn
    return jnp.clip(drawn, min=-reach, max=reach).astype(kind)


def setup_inputs(seed: int = 0, part: int = 0) -> dict:
    arg_keys = jax.random.split(jax.random.key(seed), 9)
    own_keys = jax.random.split(jax.random.fold_in(arg_keys[8], part), 9)
    state_pre = noise(own_keys[0], (NODES, D), 1.0, 4.0, ((0, 8), (1, 2)))
    loss_grad = noise(own_keys[1], (NODES, D), 1.0, 6.0, ((0, 8), (1, 2)))
    weight = noise(arg_keys[2], (D, D), D ** -0.5, 0.375, ((0, 2),))
    live_counts = uneven_parts(own_keys[3], PARTITIONS, LIVE_TOTAL, CAP, 1).astype(jnp.int32)
    partners_keys = jax.random.split(jax.random.fold_in(own_keys[4], 1), PARTITIONS * BLOCKS // BLOCKS)
    partners_turns = jax.random.permutation(jax.random.fold_in(own_keys[4], 3), PARTITIONS * BLOCKS // BLOCKS)
    partners = jax.vmap(lambda own, number: deal_out(jax.random.fold_in(own_keys[4], 2), own, number, BLOCKS, PARTITIONS, 1, MOST, 2))(partners_keys, partners_turns).reshape((PARTITIONS, BLOCKS, 1))
    row_tiles = with_ends(jax.random.randint(own_keys[5], (PARTITIONS, BLOCKS), 0, CAP // BR), jax.random.fold_in(own_keys[5], 1), 0, (CAP // BR) - 1).astype(jnp.int32)
    col_tiles = with_ends(jax.random.randint(own_keys[6], (PARTITIONS, BLOCKS), 0, CAP // BR), jax.random.fold_in(own_keys[6], 1), 0, (CAP // BR) - 1).astype(jnp.int32)
    block_tiles = noise(own_keys[7], (PARTITIONS, BLOCKS, BR, BR), (4 * BLOCKS * BR * BR // CAP) ** -0.5, 0.15625, ((0, 8),))
    return dict(state_pre=state_pre, loss_grad=loss_grad, weight=weight, live_counts=live_counts, partners=partners, row_tiles=row_tiles, col_tiles=col_tiles, block_tiles=block_tiles)


def reference(state_pre, loss_grad, weight, live_counts, partners, row_tiles, col_tiles, block_tiles):
    node_index = jnp.arange(NODES, dtype=jnp.int32)
    owner_part = node_index // CAP
    live_mask = (node_index % CAP < live_counts[owner_part]).astype(jnp.float32)[:, None]
    pre_value = state_pre.astype(jnp.float32)
    slope_term = 1.0 - jnp.tanh(pre_value) ** 2
    features = (live_mask * jnp.tanh(pre_value)).astype(jnp.bfloat16)
    feature_width = state_pre.shape[1]
    part_base = (jnp.arange(PARTITIONS, dtype=jnp.int32) * CAP)[:, None, None]
    within = jnp.arange(BR, dtype=jnp.int32)[None, None, :]
    own_rows = (part_base + row_tiles[:, :, None] * BR + within).astype(jnp.int32)
    far_rows = (partners[:, :, 0][:, :, None] * CAP + col_tiles[:, :, None] * BR + within).astype(jnp.int32)

    def forward_part(part_index, running):
        tile_values = block_tiles[part_index].astype(jnp.float32)
        gathered = features[far_rows[part_index]].astype(jnp.float32)
        contrib = jnp.einsum('kij,kjc->kic', tile_values, gathered)
        return running.at[own_rows[part_index].reshape(-1)].add(contrib.reshape(-1, feature_width))
    summed = lax.fori_loop(0, PARTITIONS, forward_part, jnp.zeros((NODES, feature_width), jnp.float32))
    gathered_sum = summed.astype(jnp.bfloat16)
    loss_value = loss_grad.astype(jnp.float32)
    adjoint = (live_mask * loss_value).astype(jnp.bfloat16)
    for iteration in range(ITERS):
        mixed_rows = jnp.dot(adjoint, weight.T, preferred_element_type=jnp.float32).astype(jnp.bfloat16)

        def backward_part(part_index, running):
            tile_values = block_tiles[part_index].astype(jnp.float32)
            picked = mixed_rows[own_rows[part_index]].astype(jnp.float32)
            message = jnp.einsum('kji,kjc->kic', tile_values, picked).astype(jnp.bfloat16)
            return running.at[far_rows[part_index].reshape(-1)].add(message.reshape(-1, feature_width).astype(jnp.float32))
        pulled = lax.fori_loop(0, PARTITIONS, backward_part, jnp.zeros((NODES, feature_width), jnp.float32))
        adjoint = (live_mask * (slope_term * pulled + loss_value)).astype(jnp.bfloat16)
    weight_grad = jnp.dot(gathered_sum.T, adjoint, preferred_element_type=jnp.float32) / math.sqrt(NODES)
    return (adjoint, weight_grad)
```

```python
import math

import jax
import jax.numpy as jnp
from jax import lax
from jax.experimental import pallas as pl
from jax.experimental.pallas import tpu as pltpu
from jax.sharding import PartitionSpec as P

ITERS = 3
VMEM_LIMIT = 48 * 1024 * 1024
PARTS = ("dom", "sub")


def trade_rows(buffer):
    return lax.all_to_all(buffer, PARTS, split_axis=0, concat_axis=0, tiled=True)


def vmem():
    return pl.BlockSpec(memory_space=pltpu.VMEM)


def smem():
    return pl.BlockSpec(memory_space=pltpu.SMEM)


def params():
    return pltpu.CompilerParams(vmem_limit_bytes=VMEM_LIMIT)


def tile_rows(index, rows):
    return pl.ds(pl.multiple_of(index * rows, rows), rows)


def request_kernel(live, wanted, state_ref, loss_ref, out_ref, grad_ref, features):
    rows = out_ref.shape[1]
    tiles = state_ref.shape[0] // rows

    @pl.loop(0, tiles)
    def _(t):
        at = tile_rows(t, rows)
        row = lax.broadcasted_iota(jnp.int32, (rows, 1), 0) + t * rows
        keep = (row < live[0]).astype(jnp.float32)
        features[t] = (keep * jnp.tanh(state_ref[at, :].astype(jnp.float32))).astype(jnp.bfloat16)
        grad_ref[at, :] = (keep * loss_ref[at, :].astype(jnp.float32)).astype(jnp.bfloat16)

    @pl.loop(0, out_ref.shape[0])
    def _(s):
        @pl.when(wanted[s] < tiles)
        def _():
            out_ref[s] = features[wanted[s]]


def message_kernel(slots, firsts, row_tiles, grad_ref, weight_ref, tiles_ref, out_ref, mixed):
    rows, columns = out_ref.shape[1:]
    tiles = grad_ref.shape[1] // rows
    step = 4 * rows

    @pl.loop(0, tiles // 4)
    def _(t):
        at = tile_rows(t, step)
        both = jnp.concatenate([grad_ref[i, at, :] for i in range(grad_ref.shape[0])], axis=1)
        mixed[at, :] = lax.dot_general(
            both, weight_ref[...], (((1,), (1,)), ((), ())), preferred_element_type=jnp.float32
        ).astype(jnp.bfloat16)

    @pl.loop(0, tiles_ref.shape[0])
    def _(k):
        @pl.when(slots[k] >= 0)
        def _():
            message = lax.dot_general(
                tiles_ref[k],
                mixed[tile_rows(row_tiles[k], rows), :],
                (((0,), (0,)), ((), ())),
                preferred_element_type=jnp.float32,
            )
            slot = slots[k]

            @pl.when(firsts[k] == 1)
            def _():
                out_ref[slot] = message.astype(jnp.bfloat16)

            @pl.when(firsts[k] == 0)
            def _():
                out_ref[slot] = (out_ref[slot].astype(jnp.float32) + message).astype(jnp.bfloat16)


def pull_kernel(live, wanted, in_ref, state_ref, loss_ref, grad_ref, pulled):
    rows = in_ref.shape[1]
    tiles = state_ref.shape[0] // rows
    pulled[...] = jnp.zeros_like(pulled)

    @pl.loop(0, in_ref.shape[0])
    def _(s):
        @pl.when(wanted[s] < tiles)
        def _():
            pulled[wanted[s]] += in_ref[s].astype(jnp.float32)

    @pl.loop(0, tiles)
    def _(t):
        at = tile_rows(t, rows)
        row = lax.broadcasted_iota(jnp.int32, (rows, 1), 0) + t * rows
        keep = (row < live[0]).astype(jnp.float32)
        slope = 1.0 - jnp.tanh(state_ref[at, :].astype(jnp.float32)) ** 2
        value = slope * pulled[t] + loss_ref[at, :].astype(jnp.float32)
        grad_ref[at, :] = (keep * value).astype(jnp.bfloat16)


def gather_kernel(slots, row_tiles, in_ref, tiles_ref, out_ref, summed):
    rows = in_ref.shape[1]
    tiles = out_ref.shape[0] // rows
    summed[...] = jnp.zeros_like(summed)

    @pl.loop(0, tiles_ref.shape[0])
    def _(k):
        @pl.when(slots[k] >= 0)
        def _():
            summed[row_tiles[k]] += jnp.dot(
                tiles_ref[k], in_ref[slots[k]], preferred_element_type=jnp.float32
            )

    @pl.loop(0, tiles)
    def _(t):
        out_ref[tile_rows(t, rows), :] = summed[t].astype(jnp.bfloat16)


def weight_kernel(sum_ref, grad_ref, out_ref):
    halves, nodes, columns = grad_ref.shape
    step = 1024 if nodes % 1024 == 0 else nodes
    out_ref[...] = jnp.zeros_like(out_ref)

    @pl.loop(0, nodes // step)
    def _(t):
        at = tile_rows(t, step)
        both = jnp.concatenate([grad_ref[i, at, :] for i in range(halves)], axis=1)
        out_ref[...] += lax.dot_general(
            sum_ref[at, :], both, (((0,), (0,)), ((), ())), preferred_element_type=jnp.float32
        )


def shards(state_pre, loss_grad, weight, live_counts, partners, row_tiles, col_tiles, block_tiles):
    node_slots, columns = state_pre.shape
    partitions = lax.axis_size("dom") * lax.axis_size("sub")
    me = lax.axis_index("dom") * lax.axis_size("sub") + lax.axis_index("sub")
    block_count = row_tiles.shape[1]
    rows = block_tiles.shape[2]
    tile_count = node_slots // rows
    capacity = max(2, 4 * block_count // (3 * partitions))
    slot_total = partitions * capacity

    with jax.named_scope("tables"):
        table = jnp.concatenate(
            [
                partners[0, :, 0],
                row_tiles[0],
                col_tiles[0],
                jnp.broadcast_to(live_counts, (128,)).astype(jnp.int32),
            ]
        )
        everyone = lax.all_gather(table, PARTS)
        partner_all = everyone[:, :block_count]
        row_all = everyone[:, block_count : 2 * block_count]
        col_all = everyone[:, 2 * block_count : 3 * block_count]
        live_tiles = (everyone[:, 3 * block_count] + rows - 1) // rows
        part_range = jnp.arange(partitions, dtype=jnp.int32)
        tile_range = jnp.arange(tile_count, dtype=jnp.int32)
        slot_range = jnp.arange(capacity, dtype=jnp.int32)
        mine = (
            (partner_all == me)
            & (row_all < live_tiles[:, None])
            & (col_all < live_tiles[me])
        )
        wants = jnp.any(mine[:, :, None] & (col_all[:, :, None] == tile_range), axis=1)
        want_place = jnp.cumsum(wants.astype(jnp.int32), axis=1) - 1
        hit = wants[:, :, None] & (want_place[:, :, None] == slot_range)
        wanted = jnp.sum(jnp.where(hit, tile_range[None, :, None], 0), axis=1)
        wanted = jnp.where(jnp.any(hit, axis=1), wanted, tile_count).reshape(slot_total)
        partner, row_tile, col_tile = partners[0, :, 0], row_tiles[0], col_tiles[0]
        partner_live = jnp.sum(
            jnp.where(partner[:, None] == part_range, live_tiles[None, :], 0), axis=1
        )
        alive = (row_tile < live_tiles[me]) & (col_tile < partner_live)
        same_partner = (partner[:, None] == partner[None, :]) & alive[None, :]
        same = same_partner & (col_tile[:, None] == col_tile[None, :])
        order = jnp.arange(block_count, dtype=jnp.int32)
        first = alive & ~jnp.any(same & (order[None, :] < order[:, None]), axis=1)
        lower = same_partner & first[None, :] & (col_tile[None, :] < col_tile[:, None])
        place = jnp.sum(lower.astype(jnp.int32), axis=1)
        slots = jnp.where(alive, partner * capacity + place, -1).astype(jnp.int32)
        firsts = first.astype(jnp.int32)

    tile_values = block_tiles[0]
    slot_shape = jax.ShapeDtypeStruct((slot_total, rows, columns), jnp.bfloat16)
    node_shape = jax.ShapeDtypeStruct((node_slots, columns), jnp.bfloat16)

    request, adjoint = pl.pallas_call(
        request_kernel,
        out_shape=(slot_shape, node_shape),
        in_specs=[smem(), smem(), vmem(), vmem()],
        out_specs=(vmem(), vmem()),
        scratch_shapes=[pltpu.VMEM((tile_count, rows, columns), jnp.bfloat16)],
        compiler_params=params(),
        name="request",
    )(live_counts, wanted, state_pre, loss_grad)
    received = trade_rows(request)
    gathered_sum = pl.pallas_call(
        gather_kernel,
        out_shape=node_shape,
        in_specs=[smem(), smem(), vmem(), vmem()],
        out_specs=vmem(),
        scratch_shapes=[pltpu.VMEM((tile_count, rows, columns), jnp.float32)],
        compiler_params=params(),
        name="gathered",
    )(slots, row_tile, received, tile_values)

    for iteration in range(ITERS):
        both = lax.all_gather(adjoint, "rep")
        outgoing = pl.pallas_call(
            message_kernel,
            out_shape=slot_shape,
            in_specs=[smem(), smem(), smem(), vmem(), vmem(), vmem()],
            out_specs=vmem(),
            scratch_shapes=[pltpu.VMEM((node_slots, columns), jnp.bfloat16)],
            compiler_params=params(),
            name="message",
        )(slots, firsts, row_tile, both, weight, tile_values)
        incoming = trade_rows(outgoing)
        adjoint = pl.pallas_call(
            pull_kernel,
            out_shape=node_shape,
            in_specs=[smem(), smem(), vmem(), vmem(), vmem()],
            out_specs=vmem(),
            scratch_shapes=[pltpu.VMEM((tile_count, rows, columns), jnp.float32)],
            compiler_params=params(),
            name="pull",
        )(live_counts, wanted, incoming, state_pre, loss_grad)

    both = lax.all_gather(adjoint, "rep")
    width = weight.shape[1]
    local_grad = pl.pallas_call(
        weight_kernel,
        out_shape=jax.ShapeDtypeStruct((columns, width), jnp.float32),
        in_specs=[vmem(), vmem()],
        out_specs=vmem(),
        compiler_params=params(),
        name="weight",
    )(gathered_sum, both)
    with jax.named_scope("total"):
        if columns % partitions == 0:
            terms = trade_rows(local_grad).reshape(partitions, columns // partitions, width)
            share = jnp.sum(terms, axis=0) / math.sqrt(node_slots * partitions)
            weight_grad = lax.all_gather(share, PARTS, axis=0, tiled=True)
        else:
            weight_grad = lax.psum(local_grad, PARTS) / math.sqrt(node_slots * partitions)
    return (adjoint, weight_grad)


def solution(mesh):
    return jax.shard_map(
        shards,
        mesh=mesh,
        in_specs=(
            P(("groups", "dom", "sub"), "rep"),
            P(("groups", "dom", "sub"), "rep"),
            P("rep", None),
            P(("groups", "dom", "sub")),
            P(("groups", "dom", "sub"), None, None),
            P(("groups", "dom", "sub"), None),
            P(("groups", "dom", "sub"), None),
            P(("groups", "dom", "sub"), None, None, None),
        ),
        out_specs=(P(("groups", "dom", "sub"), "rep"), P(("groups", "rep"), None)),
        check_vma=False,
    )
```

```python
import functools
import math

import jax
import jax.numpy as jnp
from jax import lax
from jax.experimental import pallas as pl
from jax.experimental.pallas import tpu as pltpu
from jax.sharding import PartitionSpec as P

ITERS = 3
VMEM_LIMIT = 48 * 1024 * 1024
PARTS = ("dom", "sub")
MESH = pl.DeviceIdType.MESH


def trade_rows(buffer):
    return lax.all_to_all(buffer, PARTS, split_axis=0, concat_axis=0, tiled=True)


def vmem():
    return pl.BlockSpec(memory_space=pltpu.VMEM)


def smem():
    return pl.BlockSpec(memory_space=pltpu.SMEM)


def params():
    return pltpu.CompilerParams(vmem_limit_bytes=VMEM_LIMIT)


def tile_rows(index, rows):
    return pl.ds(pl.multiple_of(index * rows, rows), rows)


def request_kernel(live, wanted, state_ref, loss_ref, out_ref, grad_ref, features):
    rows = out_ref.shape[1]
    tiles = state_ref.shape[0] // rows

    @pl.loop(0, tiles)
    def _(t):
        at = tile_rows(t, rows)
        row = lax.broadcasted_iota(jnp.int32, (rows, 1), 0) + t * rows
        keep = (row < live[0]).astype(jnp.float32)
        features[t] = (keep * jnp.tanh(state_ref[at, :].astype(jnp.float32))).astype(jnp.bfloat16)
        grad_ref[at, :] = (keep * loss_ref[at, :].astype(jnp.float32)).astype(jnp.bfloat16)

    @pl.loop(0, out_ref.shape[0])
    def _(s):
        @pl.when(wanted[s] < tiles)
        def _():
            out_ref[s] = features[wanted[s]]


def message_kernel(
    slots, firsts, row_tiles, own_ref, other_ref, weight_ref, tiles_ref, out_ref, mixed
):
    rows, columns = out_ref.shape[1:]
    tiles = own_ref.shape[0] // rows
    step = 4 * rows

    @pl.loop(0, tiles // 4)
    def _(t):
        at = tile_rows(t, step)
        both = jnp.concatenate([own_ref[at, :], other_ref[at, :]], axis=1)
        mixed[at, :] = lax.dot_general(
            both, weight_ref[...], (((1,), (1,)), ((), ())), preferred_element_type=jnp.float32
        ).astype(jnp.bfloat16)

    @pl.loop(0, tiles_ref.shape[0])
    def _(k):
        @pl.when(slots[k] >= 0)
        def _():
            message = lax.dot_general(
                tiles_ref[k],
                mixed[tile_rows(row_tiles[k], rows), :],
                (((0,), (0,)), ((), ())),
                preferred_element_type=jnp.float32,
            )
            slot = slots[k]

            @pl.when(firsts[k] == 1)
            def _():
                out_ref[slot] = message.astype(jnp.bfloat16)

            @pl.when(firsts[k] == 0)
            def _():
                out_ref[slot] = (out_ref[slot].astype(jnp.float32) + message).astype(jnp.bfloat16)


def pull_kernel(live, wanted, in_ref, state_ref, loss_ref, grad_ref, pulled):
    rows = in_ref.shape[1]
    tiles = state_ref.shape[0] // rows
    pulled[...] = jnp.zeros_like(pulled)

    @pl.loop(0, in_ref.shape[0])
    def _(s):
        @pl.when(wanted[s] < tiles)
        def _():
            pulled[wanted[s]] += in_ref[s].astype(jnp.float32)

    @pl.loop(0, tiles)
    def _(t):
        at = tile_rows(t, rows)
        row = lax.broadcasted_iota(jnp.int32, (rows, 1), 0) + t * rows
        keep = (row < live[0]).astype(jnp.float32)
        slope = 1.0 - jnp.tanh(state_ref[at, :].astype(jnp.float32)) ** 2
        value = slope * pulled[t] + loss_ref[at, :].astype(jnp.float32)
        grad_ref[at, :] = (keep * value).astype(jnp.bfloat16)


def gather_kernel(slots, row_tiles, in_ref, tiles_ref, out_ref, summed):
    rows = in_ref.shape[1]
    tiles = out_ref.shape[0] // rows
    summed[...] = jnp.zeros_like(summed)

    @pl.loop(0, tiles_ref.shape[0])
    def _(k):
        @pl.when(slots[k] >= 0)
        def _():
            summed[row_tiles[k]] += jnp.dot(
                tiles_ref[k], in_ref[slots[k]], preferred_element_type=jnp.float32
            )

    @pl.loop(0, tiles)
    def _(t):
        out_ref[tile_rows(t, rows), :] = summed[t].astype(jnp.bfloat16)


def peer_of(number):
    sub = lax.axis_size("sub")
    return {"dom": number // sub, "sub": lax.rem(number, sub)}


def position():
    return lax.axis_index("dom") * lax.axis_size("sub") + lax.axis_index("sub")


def greet(devices):
    barrier = pltpu.get_barrier_semaphore()
    for device in devices:
        pl.semaphore_signal(barrier, inc=1, device_id=device, device_id_type=MESH)
    pl.semaphore_wait(barrier, len(devices))


def remote(src, dst, send_sem, recv_sem, device):
    return pltpu.make_async_remote_copy(
        src_ref=src,
        dst_ref=dst,
        send_sem=send_sem,
        recv_sem=recv_sem,
        device_id=device,
        device_id_type=MESH,
    )


def table_kernel(in_ref, out_ref, send_sem, recv_sem, own_sem):
    groups, parts = out_ref.shape[0], out_ref.shape[1]
    group, me = lax.axis_index("groups"), position()
    others = []
    for turn in range(1, groups * parts):
        place = lax.rem(group * parts + me + turn, groups * parts)
        device = {"groups": place // parts, **peer_of(lax.rem(place, parts))}
        others.append(device)
    greet(others)
    copies = [
        remote(in_ref, out_ref.at[group, me], send_sem.at[i], recv_sem.at[i], device)
        for i, device in enumerate(others)
    ]
    for copy in copies:
        copy.start()
    own = pltpu.make_async_copy(in_ref, out_ref.at[group, me], own_sem)
    own.start()
    own.wait()
    for copy in copies:
        copy.wait()


def table_gather(table, groups, parts):
    count = groups * parts - 1
    return pl.pallas_call(
        table_kernel,
        out_shape=jax.ShapeDtypeStruct((groups, parts) + table.shape, table.dtype),
        in_specs=[vmem()],
        out_specs=vmem(),
        scratch_shapes=[
            pltpu.SemaphoreType.DMA((count,)),
            pltpu.SemaphoreType.DMA((count,)),
            pltpu.SemaphoreType.DMA,
        ],
        compiler_params=pltpu.CompilerParams(collective_id=0, has_side_effects=True),
        name="tables",
    )(table)


def trade_kernel(parts, capacity, count, in_ref, out_ref, send_sem, recv_sem, own_sem):
    me = position()
    turns = far_first(parts)
    targets = [lax.rem(me + turn, parts) for turn in turns]
    greet([peer_of(target) for target in targets])
    copies = [
        remote(
            in_ref.at[pl.ds(target * capacity, count)],
            out_ref.at[pl.ds(me * capacity, count)],
            send_sem.at[i],
            recv_sem.at[i],
            peer_of(target),
        )
        for i, target in enumerate(targets)
    ]
    for copy in copies:
        copy.start()
    own = pltpu.make_async_copy(
        in_ref.at[pl.ds(me * capacity, capacity)],
        out_ref.at[pl.ds(me * capacity, capacity)],
        own_sem,
    )
    own.start()
    own.wait()
    for copy in copies:
        copy.wait()


def far_first(parts):
    return sorted(range(1, parts), key=lambda turn: -min(turn, parts - turn))


def trade_some(buffer, parts, count, identity):
    capacity = buffer.shape[0] // parts
    return pl.pallas_call(
        functools.partial(trade_kernel, parts, capacity, count),
        out_shape=jax.ShapeDtypeStruct(buffer.shape, buffer.dtype),
        in_specs=[pl.BlockSpec(memory_space=pl.ANY)],
        out_specs=pl.BlockSpec(memory_space=pl.ANY),
        scratch_shapes=[
            pltpu.SemaphoreType.DMA((parts - 1,)),
            pltpu.SemaphoreType.DMA((parts - 1,)),
            pltpu.SemaphoreType.DMA,
        ],
        compiler_params=pltpu.CompilerParams(collective_id=identity, has_side_effects=True),
        name="trade",
    )(buffer)


def trade_slots(buffer, parts, busiest):
    capacity = buffer.shape[0] // parts
    counts = list(range(max(1, capacity - 4), capacity + 1))
    branches = [
        functools.partial(trade_some, parts=parts, count=count, identity=3 + i)
        for i, count in enumerate(counts)
    ]
    return lax.switch(jnp.clip(busiest - counts[0], 0, len(counts) - 1), branches, buffer)


def swap_kernel(in_ref, out_ref, send_sem, recv_sem):
    other = {"rep": 1 - lax.axis_index("rep")}
    greet([other])
    copy = remote(in_ref, out_ref, send_sem, recv_sem, other)
    copy.start()
    copy.wait()


def swap(array):
    return pl.pallas_call(
        swap_kernel,
        out_shape=jax.ShapeDtypeStruct(array.shape, array.dtype),
        in_specs=[pl.BlockSpec(memory_space=pl.ANY)],
        out_specs=pl.BlockSpec(memory_space=pl.ANY),
        scratch_shapes=[pltpu.SemaphoreType.DMA, pltpu.SemaphoreType.DMA],
        compiler_params=pltpu.CompilerParams(collective_id=1, has_side_effects=True),
        name="swap",
    )(array)


def columns_product(sum_ref, grad_ref):
    nodes = sum_ref.shape[0]
    step = 1024 if nodes % 1024 == 0 else nodes

    def add(t, total):
        at = tile_rows(t, step)
        return total + lax.dot_general(
            sum_ref[at, :], grad_ref[at, :], (((0,), (0,)), ((), ())),
            preferred_element_type=jnp.float32,
        )

    zero = jnp.zeros((sum_ref.shape[1], grad_ref.shape[1]), jnp.float32)
    return lax.fori_loop(0, nodes // step, add, zero)


def total_kernel(
    scale, sum_ref, grad_ref, out_ref, other, local, terms, share, parted,
    swap_sem, send_sem, recv_sem, send_again, recv_again,
):
    parts, _, rows, columns = terms.shape
    me, rep = position(), lax.axis_index("rep")
    targets = [lax.rem(me + turn, parts) for turn in far_first(parts)]
    peers = [peer_of(target) for target in targets]
    core = {"rep": 1 - rep}
    greet(peers + [core])
    swapped = remote(grad_ref, other, swap_sem.at[0], swap_sem.at[1], core)
    swapped.start()
    local[rep] = columns_product(sum_ref, grad_ref)
    swapped.wait()
    local[1 - rep] = columns_product(sum_ref, other)

    def rows_of(number):
        return pl.ds(pl.multiple_of(number * rows, rows), rows)

    copies = [
        remote(
            local.at[:, rows_of(target), :], terms.at[me], send_sem.at[i], recv_sem.at[i], peer
        )
        for i, (target, peer) in enumerate(zip(targets, peers))
    ]
    for copy in copies:
        copy.start()
    terms[me] = local[:, rows_of(me), :]
    for copy in copies:
        copy.wait()
    share[...] = jnp.sum(terms[...], axis=0) * scale
    copies = [
        remote(share, parted.at[me], send_again.at[i], recv_again.at[i], peer)
        for i, peer in enumerate(peers)
    ]
    for copy in copies:
        copy.start()
    parted[me] = share[...]
    for copy in copies:
        copy.wait()
    for part in range(parts):
        for half in range(2):
            out_ref[part * rows : (part + 1) * rows, half * columns : (half + 1) * columns] = (
                parted[part, half]
            )


def total_grad(gathered_sum, adjoint, parts):
    nodes, columns = adjoint.shape
    rows = columns // parts
    return pl.pallas_call(
        functools.partial(total_kernel, 1.0 / math.sqrt(nodes * parts)),
        out_shape=jax.ShapeDtypeStruct((columns, 2 * columns), jnp.float32),
        in_specs=[vmem(), vmem()],
        out_specs=vmem(),
        scratch_shapes=[
            pltpu.VMEM((nodes, columns), jnp.bfloat16),
            pltpu.VMEM((2, columns, columns), jnp.float32),
            pltpu.VMEM((parts, 2, rows, columns), jnp.float32),
            pltpu.VMEM((2, rows, columns), jnp.float32),
            pltpu.VMEM((parts, 2, rows, columns), jnp.float32),
            pltpu.SemaphoreType.DMA((2,)),
        ]
        + [pltpu.SemaphoreType.DMA((parts - 1,))] * 4,
        compiler_params=pltpu.CompilerParams(
            collective_id=2, has_side_effects=True, vmem_limit_bytes=VMEM_LIMIT
        ),
        name="total",
    )(gathered_sum, adjoint)


def shards(state_pre, loss_grad, weight, live_counts, partners, row_tiles, col_tiles, block_tiles):
    node_slots, columns = state_pre.shape
    partitions = lax.axis_size("dom") * lax.axis_size("sub")
    groups = lax.axis_size("groups")
    me = position()
    near = partitions <= 16 and columns % (8 * partitions) == 0
    block_count = row_tiles.shape[1]
    rows = block_tiles.shape[2]
    tile_count = node_slots // rows
    capacity = max(2, 4 * block_count // (3 * partitions))
    slot_total = partitions * capacity

    with jax.named_scope("tables"):
        table = jnp.stack(
            [
                jnp.pad(row, (0, -row.shape[0] % 128))
                for row in (
                    partners[0, :, 0],
                    row_tiles[0],
                    col_tiles[0],
                    jnp.broadcast_to(live_counts, (block_count,)),
                )
            ]
        )
        table = jnp.pad(table, ((0, 4), (0, 0)))
        if near:
            everyone = table_gather(table, groups, partitions)
        else:
            everyone = lax.all_gather(table, PARTS)[None]
        live_everywhere = (everyone[:, :, 3, 0] + rows - 1) // rows
        part_range = jnp.arange(partitions, dtype=jnp.int32)
        if near:
            group = lax.axis_index("groups")
            partner_each = everyone[:, :, 0, :block_count, None] == part_range
            partner_live = jnp.sum(
                jnp.where(partner_each, live_everywhere[:, None, None, :], 0), axis=3
            )
            alive_each = (everyone[:, :, 1, :block_count] < live_everywhere[:, :, None]) & (
                everyone[:, :, 2, :block_count] < partner_live
            )
            col_each = everyone[:, :, 2, :block_count, None] == jnp.arange(tile_count)
            used = jnp.einsum(
                "gpkq,gpkt->gpqt",
                (partner_each & alive_each[..., None]).astype(jnp.bfloat16),
                col_each.astype(jnp.bfloat16),
                preferred_element_type=jnp.float32,
            )
            away = part_range[:, None] != part_range[None, :]
            tiles_used = jnp.sum((used > 0).astype(jnp.int32), axis=3)
            busiest = jnp.max(jnp.where(away[None], tiles_used, 0))
        else:
            group, busiest = 0, capacity
        everyone = lax.dynamic_index_in_dim(everyone, group, 0, keepdims=False)
        live_tiles = lax.dynamic_index_in_dim(live_everywhere, group, 0, keepdims=False)
        partner_all = everyone[:, 0, :block_count]
        row_all = everyone[:, 1, :block_count]
        col_all = everyone[:, 2, :block_count]
        tile_range = jnp.arange(tile_count, dtype=jnp.int32)
        slot_range = jnp.arange(capacity, dtype=jnp.int32)
        mine = (
            (partner_all == me)
            & (row_all < live_tiles[:, None])
            & (col_all < live_tiles[me])
        )
        wants = jnp.any(mine[:, :, None] & (col_all[:, :, None] == tile_range), axis=1)
        want_place = jnp.cumsum(wants.astype(jnp.int32), axis=1) - 1
        hit = wants[:, :, None] & (want_place[:, :, None] == slot_range)
        wanted = jnp.sum(jnp.where(hit, tile_range[None, :, None], 0), axis=1)
        wanted = jnp.where(jnp.any(hit, axis=1), wanted, tile_count).reshape(slot_total)
        partner, row_tile, col_tile = partners[0, :, 0], row_tiles[0], col_tiles[0]
        partner_live = jnp.sum(
            jnp.where(partner[:, None] == part_range, live_tiles[None, :], 0), axis=1
        )
        alive = (row_tile < live_tiles[me]) & (col_tile < partner_live)
        same_partner = (partner[:, None] == partner[None, :]) & alive[None, :]
        same = same_partner & (col_tile[:, None] == col_tile[None, :])
        order = jnp.arange(block_count, dtype=jnp.int32)
        first = alive & ~jnp.any(same & (order[None, :] < order[:, None]), axis=1)
        lower = same_partner & first[None, :] & (col_tile[None, :] < col_tile[:, None])
        place = jnp.sum(lower.astype(jnp.int32), axis=1)
        slots = jnp.where(alive, partner * capacity + place, -1).astype(jnp.int32)
        firsts = first.astype(jnp.int32)

    tile_values = block_tiles[0]
    slot_shape = jax.ShapeDtypeStruct((slot_total, rows, columns), jnp.bfloat16)
    node_shape = jax.ShapeDtypeStruct((node_slots, columns), jnp.bfloat16)

    request, adjoint = pl.pallas_call(
        request_kernel,
        out_shape=(slot_shape, node_shape),
        in_specs=[smem(), smem(), vmem(), vmem()],
        out_specs=(vmem(), vmem()),
        scratch_shapes=[pltpu.VMEM((tile_count, rows, columns), jnp.bfloat16)],
        compiler_params=params(),
        name="request",
    )(live_counts, wanted, state_pre, loss_grad)
    def exchange(buffer):
        return trade_slots(buffer, partitions, busiest) if near else trade_rows(buffer)

    rep = lax.axis_index("rep")
    halves = [
        lax.dynamic_slice_in_dim(weight, half * columns, columns, 1) for half in (rep, 1 - rep)
    ]
    own_weight = jnp.concatenate(halves, axis=1)
    received = exchange(request)
    gathered_sum = pl.pallas_call(
        gather_kernel,
        out_shape=node_shape,
        in_specs=[smem(), smem(), vmem(), vmem()],
        out_specs=vmem(),
        scratch_shapes=[pltpu.VMEM((tile_count, rows, columns), jnp.float32)],
        compiler_params=params(),
        name="gathered",
    )(slots, row_tile, received, tile_values)

    for iteration in range(ITERS):
        other = swap(adjoint)
        outgoing = pl.pallas_call(
            message_kernel,
            out_shape=slot_shape,
            in_specs=[smem(), smem(), smem(), vmem(), vmem(), vmem(), vmem()],
            out_specs=vmem(),
            scratch_shapes=[pltpu.VMEM((node_slots, columns), jnp.bfloat16)],
            compiler_params=params(),
            name="message",
        )(slots, firsts, row_tile, adjoint, other, own_weight, tile_values)
        incoming = exchange(outgoing)
        adjoint = pl.pallas_call(
            pull_kernel,
            out_shape=node_shape,
            in_specs=[smem(), smem(), vmem(), vmem(), vmem()],
            out_specs=vmem(),
            scratch_shapes=[pltpu.VMEM((tile_count, rows, columns), jnp.float32)],
            compiler_params=params(),
            name="pull",
        )(live_counts, wanted, incoming, state_pre, loss_grad)

    if near:
        return (adjoint, total_grad(gathered_sum, adjoint, partitions))
    local_grad = lax.dot_general(
        gathered_sum,
        lax.all_gather(adjoint, "rep", axis=1, tiled=True),
        (((0,), (0,)), ((), ())),
        preferred_element_type=jnp.float32,
    )
    weight_grad = lax.psum(local_grad, PARTS) / math.sqrt(node_slots * partitions)
    return (adjoint, weight_grad)


def solution(mesh):
    return jax.shard_map(
        shards,
        mesh=mesh,
        in_specs=(
            P(("groups", "dom", "sub"), "rep"),
            P(("groups", "dom", "sub"), "rep"),
            P("rep", None),
            P(("groups", "dom", "sub")),
            P(("groups", "dom", "sub"), None, None),
            P(("groups", "dom", "sub"), None),
            P(("groups", "dom", "sub"), None),
            P(("groups", "dom", "sub"), None, None, None),
        ),
        out_specs=(P(("groups", "dom", "sub"), "rep"), P(("groups", "rep"), None)),
        check_vma=False,
    )
```

```python
import functools
import math

import jax
import jax.numpy as jnp
from jax import lax
from jax.experimental import pallas as pl
from jax.experimental.pallas import tpu as pltpu
from jax.sharding import PartitionSpec as P

ITERS = 3
VMEM_LIMIT = 48 * 1024 * 1024
PARTS = ("dom", "sub")
MESH = pl.DeviceIdType.MESH


def trade_rows(buffer):
    return lax.all_to_all(buffer, PARTS, split_axis=0, concat_axis=0, tiled=True)


def vmem():
    return pl.BlockSpec(memory_space=pltpu.VMEM)


def smem():
    return pl.BlockSpec(memory_space=pltpu.SMEM)


def params():
    return pltpu.CompilerParams(vmem_limit_bytes=VMEM_LIMIT)


def tile_rows(index, rows):
    return pl.ds(pl.multiple_of(index * rows, rows), rows)


def request_kernel(live, wanted, state_ref, loss_ref, out_ref, grad_ref, features):
    rows = out_ref.shape[1]
    tiles = state_ref.shape[0] // rows

    @pl.loop(0, tiles)
    def _(t):
        at = tile_rows(t, rows)
        row = lax.broadcasted_iota(jnp.int32, (rows, 1), 0) + t * rows
        keep = (row < live[0]).astype(jnp.float32)
        features[t] = (keep * jnp.tanh(state_ref[at, :].astype(jnp.float32))).astype(jnp.bfloat16)
        grad_ref[at, :] = (keep * loss_ref[at, :].astype(jnp.float32)).astype(jnp.bfloat16)

    @pl.loop(0, out_ref.shape[0])
    def _(s):
        @pl.when(wanted[s] < tiles)
        def _():
            out_ref[s] = features[wanted[s]]


def message_kernel(
    slots, firsts, row_tiles, own_ref, other_ref, weight_ref, tiles_ref, out_ref, mixed
):
    rows, columns = out_ref.shape[1:]
    tiles = own_ref.shape[0] // rows
    step = 4 * rows

    @pl.loop(0, tiles // 4)
    def _(t):
        at = tile_rows(t, step)
        both = jnp.concatenate([own_ref[at, :], other_ref[at, :]], axis=1)
        mixed[at, :] = lax.dot_general(
            both, weight_ref[...], (((1,), (1,)), ((), ())), preferred_element_type=jnp.float32
        ).astype(jnp.bfloat16)

    @pl.loop(0, tiles_ref.shape[0])
    def _(k):
        @pl.when(slots[k] >= 0)
        def _():
            message = lax.dot_general(
                tiles_ref[k],
                mixed[tile_rows(row_tiles[k], rows), :],
                (((0,), (0,)), ((), ())),
                preferred_element_type=jnp.float32,
            )
            slot = slots[k]

            @pl.when(firsts[k] == 1)
            def _():
                out_ref[slot] = message.astype(jnp.bfloat16)

            @pl.when(firsts[k] == 0)
            def _():
                out_ref[slot] = (out_ref[slot].astype(jnp.float32) + message).astype(jnp.bfloat16)


def pull_kernel(live, wanted, in_ref, state_ref, loss_ref, grad_ref, pulled):
    rows = in_ref.shape[1]
    tiles = state_ref.shape[0] // rows
    pulled[...] = jnp.zeros_like(pulled)

    @pl.loop(0, in_ref.shape[0])
    def _(s):
        @pl.when(wanted[s] < tiles)
        def _():
            pulled[wanted[s]] += in_ref[s].astype(jnp.float32)

    @pl.loop(0, tiles)
    def _(t):
        at = tile_rows(t, rows)
        row = lax.broadcasted_iota(jnp.int32, (rows, 1), 0) + t * rows
        keep = (row < live[0]).astype(jnp.float32)
        slope = 1.0 - jnp.tanh(state_ref[at, :].astype(jnp.float32)) ** 2
        value = slope * pulled[t] + loss_ref[at, :].astype(jnp.float32)
        grad_ref[at, :] = (keep * value).astype(jnp.bfloat16)


def gather_kernel(slots, row_tiles, in_ref, tiles_ref, out_ref, summed):
    rows = in_ref.shape[1]
    tiles = out_ref.shape[0] // rows
    summed[...] = jnp.zeros_like(summed)

    @pl.loop(0, tiles_ref.shape[0])
    def _(k):
        @pl.when(slots[k] >= 0)
        def _():
            summed[row_tiles[k]] += jnp.dot(
                tiles_ref[k], in_ref[slots[k]], preferred_element_type=jnp.float32
            )

    @pl.loop(0, tiles)
    def _(t):
        out_ref[tile_rows(t, rows), :] = summed[t].astype(jnp.bfloat16)


def peer_of(number):
    sub = lax.axis_size("sub")
    return {"dom": number // sub, "sub": lax.rem(number, sub)}


def position():
    return lax.axis_index("dom") * lax.axis_size("sub") + lax.axis_index("sub")


def greet(devices):
    barrier = pltpu.get_barrier_semaphore()
    for device in devices:
        pl.semaphore_signal(barrier, inc=1, device_id=device, device_id_type=MESH)
    pl.semaphore_wait(barrier, len(devices))


def remote(src, dst, send_sem, recv_sem, device):
    return pltpu.make_async_remote_copy(
        src_ref=src,
        dst_ref=dst,
        send_sem=send_sem,
        recv_sem=recv_sem,
        device_id=device,
        device_id_type=MESH,
    )


def table_kernel(in_ref, out_ref, send_sem, recv_sem, own_sem):
    groups, parts = out_ref.shape[0], out_ref.shape[1]
    group, me = lax.axis_index("groups"), position()
    others = []
    for turn in range(1, groups * parts):
        place = lax.rem(group * parts + me + turn, groups * parts)
        device = {"groups": place // parts, **peer_of(lax.rem(place, parts))}
        others.append(device)
    greet(others)
    copies = [
        remote(in_ref, out_ref.at[group, me], send_sem.at[i], recv_sem.at[i], device)
        for i, device in enumerate(others)
    ]
    for copy in copies:
        copy.start()
    own = pltpu.make_async_copy(in_ref, out_ref.at[group, me], own_sem)
    own.start()
    own.wait()
    for copy in copies:
        copy.wait()


def table_gather(table, groups, parts):
    count = groups * parts - 1
    return pl.pallas_call(
        table_kernel,
        out_shape=jax.ShapeDtypeStruct((groups, parts) + table.shape, table.dtype),
        in_specs=[vmem()],
        out_specs=vmem(),
        scratch_shapes=[
            pltpu.SemaphoreType.DMA((count,)),
            pltpu.SemaphoreType.DMA((count,)),
            pltpu.SemaphoreType.DMA,
        ],
        compiler_params=pltpu.CompilerParams(collective_id=0, has_side_effects=True),
        name="tables",
    )(table)


def turns_of(dom, sub):
    ahead = sorted(range(dom), key=lambda turn: -min(turn, dom - turn))
    return [(dz, dx) for dz in ahead for dx in range(sub) if dz or dx]


def whole_kernel(
    count, capacity, scale, turns, live, want_tile, in_place, block_at, row_at, same_at, last_at,
    sum_block, sum_slot, sum_same, sum_last, state_ref, loss_ref, weight_ref, tiles_any,
    grad_ref, total_ref,
    tiles, turned, features, slope, other, mixed, segment, outgoing, incoming_even, incoming_odd, request,
    arrived,
    running, summed, local, terms, share, parted,
    tile_sem, swap_send, swap_recv, send_sem, recv_sem, ask_send, ask_recv, sum_send, sum_recv,
    part_send, part_recv,
):
    blocks, rows, columns = tiles.shape
    nodes = state_ref.shape[0]
    tile_count = nodes // rows
    dom, sub = lax.axis_size("dom"), lax.axis_size("sub")
    parts = dom * sub
    z, x, rep = lax.axis_index("dom"), lax.axis_index("sub"), lax.axis_index("rep")
    me = z * sub + x
    peers, targets = [], []
    for dz, dx in turns:
        far = {"dom": lax.rem(z + dz, dom), "sub": lax.rem(x + dx, sub)}
        peers.append(far)
        targets.append(far["dom"] * sub + far["sub"])
    core = {"rep": 1 - rep}
    fetch = pltpu.make_async_copy(tiles_any, tiles, tile_sem)
    fetch.start()
    greet(peers + [core])
    quarters = 4
    incoming = (incoming_even, incoming_odd)
    quarter = nodes // quarters

    def swap_copy(turn, part):
        at = pl.ds(part * quarter, quarter)
        return remote(
            grad_ref.at[at],
            other.at[turn % 2, at],
            swap_send.at[turn, part],
            swap_recv.at[turn, part],
            core,
        )

    def keep_of(t):
        row = lax.broadcasted_iota(jnp.int32, (rows, 1), 0) + t * rows
        return (row < live[0]).astype(jnp.float32)

    for part in range(quarters):

        @pl.loop(part * tile_count // quarters, (part + 1) * tile_count // quarters)
        def _(t):
            at = tile_rows(t, rows)
            grad_ref[at, :] = (keep_of(t) * loss_ref[at, :].astype(jnp.float32)).astype(
                jnp.bfloat16
            )

        swap_copy(0, part).start()

    @pl.loop(0, tile_count)
    def _(t):
        at = tile_rows(t, rows)
        value = jnp.tanh(state_ref[at, :].astype(jnp.float32))
        features[t] = (keep_of(t) * value).astype(jnp.bfloat16)
        slope[t] = 1.0 - value * value

    fetch.wait()

    @pl.loop(0, blocks, unroll=2)
    def _(k):
        turned[k] = tiles[k].T

    def ask(i):
        target = targets[i]

        @pl.loop(0, count)
        def _(s):
            request[target, s] = features[want_tile[target * capacity + s]]

        remote(
            request.at[target, pl.ds(0, count)],
            arrived.at[me, pl.ds(0, count)],
            ask_send.at[i],
            ask_recv.at[i],
            peers[i],
        ).start()

    def ask_copy(i):
        return remote(
            request.at[targets[i], pl.ds(0, count)],
            arrived.at[me, pl.ds(0, count)],
            ask_send.at[i],
            ask_recv.at[i],
            peers[i],
        )

    def messages_to(target, into):
        def add(j, total):
            at = target * capacity + j
            message = jnp.dot(
                turned[block_at[at]], mixed[row_at[at]], preferred_element_type=jnp.float32
            )
            total = jnp.where(same_at[at] > 0, total, 0.0) + message
            segment[j] = total.astype(jnp.bfloat16)
            return total

        lax.fori_loop(0, capacity, add, jnp.zeros((rows, columns), jnp.float32), unroll=4)

        @pl.loop(0, count if into is outgoing else capacity)
        def _(s):
            into[target, s] = segment[last_at[target * capacity + s]]

    def send_copy(turn, i):
        return remote(
            outgoing.at[targets[i], pl.ds(0, count)],
            incoming[turn % 2].at[me, pl.ds(0, count)],
            send_sem.at[turn, i],
            recv_sem.at[turn, i],
            peers[i],
        )

    many = len(turns)
    half = (many + 1) // 2
    for turn in range(ITERS):
        step = quarter // rows
        for part in range(quarters):
            swap_copy(turn, part).wait()

            @pl.loop(part * step, (part + 1) * step)
            def _(t):
                at = tile_rows(t, rows)
                both = jnp.concatenate([grad_ref[at, :], other[turn % 2, at, :]], axis=1)
                mixed[t] = lax.dot_general(
                    both,
                    weight_ref[...],
                    (((1,), (1,)), ((), ())),
                    preferred_element_type=jnp.float32,
                ).astype(jnp.bfloat16)

        for i in range(many):
            messages_to(targets[i], outgoing)
            send_copy(turn, i).start()
        messages_to(me, incoming[turn % 2])
        if turn == 0:
            for i in range(half):
                ask(i)
        elif turn == 1:
            for i in range(half, many):
                ask(i)

            @pl.loop(0, capacity)
            def _(s):
                arrived[me, s] = features[want_tile[me * capacity + s]]

        else:
            for i in range(many):
                ask_copy(i).wait()

            def add(j, total):
                slot = sum_slot[j]
                product = jnp.dot(
                    tiles[sum_block[j]],
                    arrived[slot // capacity, lax.rem(slot, capacity)],
                    preferred_element_type=jnp.float32,
                )
                total = jnp.where(sum_same[j] > 0, total, 0.0) + product
                running[j] = total
                return total

            lax.fori_loop(0, blocks, add, jnp.zeros((rows, columns), jnp.float32), unroll=4)

            @pl.loop(0, tile_count)
            def _(t):
                last = sum_last[t]
                value = jnp.where(last >= 0, running[jnp.maximum(last, 0)], 0.0)
                summed[tile_rows(t, rows), :] = value.astype(jnp.bfloat16)

        for i in range(many):
            send_copy(turn, i).wait()
        for part in range(quarters):

            @pl.loop(part * step, (part + 1) * step)
            def _(t):
                at = tile_rows(t, rows)
                total = jnp.zeros((rows, columns), jnp.float32)
                for source in range(parts):
                    place = in_place[source * tile_count + t]
                    value = incoming[turn % 2][source, jnp.maximum(place, 0)]
                    total = total + jnp.where(place >= 0, value.astype(jnp.float32), 0.0)
                value = slope[t] * total + loss_ref[at, :].astype(jnp.float32)
                grad_ref[at, :] = (keep_of(t) * value).astype(jnp.bfloat16)

            swap_copy(turn + 1, part).start()

    local[rep] = columns_product(summed, grad_ref)
    for part in range(quarters):
        swap_copy(ITERS, part).wait()
    local[1 - rep] = columns_product(summed, other.at[ITERS % 2])
    share_rows = columns // parts

    def rows_of(number):
        return pl.ds(pl.multiple_of(number * share_rows, share_rows), share_rows)

    copies = [
        remote(
            local.at[:, rows_of(target), :], terms.at[me], sum_send.at[i], sum_recv.at[i], peer
        )
        for i, (target, peer) in enumerate(zip(targets, peers))
    ]
    for copy in copies:
        copy.start()
    terms[me] = local[:, rows_of(me), :]
    for copy in copies:
        copy.wait()
    share[...] = jnp.sum(terms[...], axis=0) * scale
    copies = [
        remote(share, parted.at[me], part_send.at[i], part_recv.at[i], peer)
        for i, peer in enumerate(peers)
    ]
    for copy in copies:
        copy.start()
    parted[me] = share[...]
    for copy in copies:
        copy.wait()
    for part in range(parts):
        for side in range(2):
            total_ref[
                part * share_rows : (part + 1) * share_rows, side * columns : (side + 1) * columns
            ] = parted[part, side]


def whole(*operands, parts, turns, capacity, count, identity):
    state_pre, tile_values = operands[-4], operands[-1]
    nodes, columns = state_pre.shape
    blocks, rows, _ = tile_values.shape
    tile_count = nodes // rows
    many = len(turns)
    slots = (parts, capacity, rows, columns)
    dma = pltpu.SemaphoreType.DMA
    return pl.pallas_call(
        functools.partial(
            whole_kernel, count, capacity, 1.0 / math.sqrt(nodes * parts), turns
        ),
        out_shape=(
            jax.ShapeDtypeStruct((nodes, columns), jnp.bfloat16),
            jax.ShapeDtypeStruct((columns, 2 * columns), jnp.float32),
        ),
        in_specs=[smem()] * (len(operands) - 4)
        + [vmem()] * 3
        + [pl.BlockSpec(memory_space=pl.ANY)],
        out_specs=(vmem(), vmem()),
        scratch_shapes=[
            pltpu.VMEM((blocks, rows, rows), jnp.bfloat16),
            pltpu.VMEM((blocks, rows, rows), jnp.bfloat16),
            pltpu.VMEM((tile_count, rows, columns), jnp.bfloat16),
            pltpu.VMEM((tile_count, rows, columns), jnp.float32),
            pltpu.VMEM((2, nodes, columns), jnp.bfloat16),
            pltpu.VMEM((tile_count, rows, columns), jnp.bfloat16),
            pltpu.VMEM((capacity, rows, columns), jnp.bfloat16),
            pltpu.VMEM(slots, jnp.bfloat16),
            pltpu.VMEM(slots, jnp.bfloat16),
            pltpu.VMEM(slots, jnp.bfloat16),
            pltpu.VMEM(slots, jnp.bfloat16),
            pltpu.VMEM(slots, jnp.bfloat16),
            pltpu.VMEM((blocks, rows, columns), jnp.float32),
            pltpu.VMEM((nodes, columns), jnp.bfloat16),
            pltpu.VMEM((2, columns, columns), jnp.float32),
            pltpu.VMEM((parts, 2, columns // parts, columns), jnp.float32),
            pltpu.VMEM((2, columns // parts, columns), jnp.float32),
            pltpu.VMEM((parts, 2, columns // parts, columns), jnp.float32),
            dma,
            dma((ITERS + 1, 4)),
            dma((ITERS + 1, 4)),
            dma((ITERS, many)),
            dma((ITERS, many)),
            dma((many,)),
            dma((many,)),
            dma((many,)),
            dma((many,)),
            dma((many,)),
            dma((many,)),
        ],
        compiler_params=pltpu.CompilerParams(
            collective_id=identity, has_side_effects=True, vmem_limit_bytes=60 * 1024 * 1024
        ),
        name="whole",
    )(*operands)


def swap_kernel(in_ref, out_ref, send_sem, recv_sem):
    other = {"rep": 1 - lax.axis_index("rep")}
    greet([other])
    copy = remote(in_ref, out_ref, send_sem, recv_sem, other)
    copy.start()
    copy.wait()


def swap(array):
    return pl.pallas_call(
        swap_kernel,
        out_shape=jax.ShapeDtypeStruct(array.shape, array.dtype),
        in_specs=[pl.BlockSpec(memory_space=pl.ANY)],
        out_specs=pl.BlockSpec(memory_space=pl.ANY),
        scratch_shapes=[pltpu.SemaphoreType.DMA, pltpu.SemaphoreType.DMA],
        compiler_params=pltpu.CompilerParams(collective_id=1, has_side_effects=True),
        name="swap",
    )(array)


def columns_product(sum_ref, grad_ref):
    nodes = sum_ref.shape[0]
    step = 1024 if nodes % 1024 == 0 else nodes

    def add(t, total):
        at = tile_rows(t, step)
        return total + lax.dot_general(
            sum_ref[at, :], grad_ref[at, :], (((0,), (0,)), ((), ())),
            preferred_element_type=jnp.float32,
        )

    zero = jnp.zeros((sum_ref.shape[1], grad_ref.shape[1]), jnp.float32)
    return lax.fori_loop(0, nodes // step, add, zero)


def shards(state_pre, loss_grad, weight, live_counts, partners, row_tiles, col_tiles, block_tiles):
    node_slots, columns = state_pre.shape
    partitions = lax.axis_size("dom") * lax.axis_size("sub")
    groups = lax.axis_size("groups")
    me = position()
    near = partitions <= 16 and columns % (8 * partitions) == 0
    block_count = row_tiles.shape[1]
    rows = block_tiles.shape[2]
    tile_count = node_slots // rows
    capacity = max(2, 4 * block_count // (3 * partitions))
    slot_total = partitions * capacity

    with jax.named_scope("tables"):
        table = jnp.stack(
            [
                jnp.pad(row, (0, -row.shape[0] % 128))
                for row in (
                    partners[0, :, 0],
                    row_tiles[0],
                    col_tiles[0],
                    jnp.broadcast_to(live_counts, (block_count,)),
                )
            ]
        )
        table = jnp.pad(table, ((0, 4), (0, 0)))
        if near:
            everyone = table_gather(table, groups, partitions)
        else:
            everyone = lax.all_gather(table, PARTS)[None]
        live_everywhere = (everyone[:, :, 3, 0] + rows - 1) // rows
        part_range = jnp.arange(partitions, dtype=jnp.int32)
        if near:
            group = lax.axis_index("groups")
            partner_each = everyone[:, :, 0, :block_count, None] == part_range
            partner_live = jnp.sum(
                jnp.where(partner_each, live_everywhere[:, None, None, :], 0), axis=3
            )
            alive_each = (everyone[:, :, 1, :block_count] < live_everywhere[:, :, None]) & (
                everyone[:, :, 2, :block_count] < partner_live
            )
            col_each = everyone[:, :, 2, :block_count, None] == jnp.arange(tile_count)
            used = jnp.einsum(
                "gpkq,gpkt->gpqt",
                (partner_each & alive_each[..., None]).astype(jnp.bfloat16),
                col_each.astype(jnp.bfloat16),
                preferred_element_type=jnp.float32,
            )
            away = part_range[:, None] != part_range[None, :]
            tiles_used = jnp.sum((used > 0).astype(jnp.int32), axis=3)
            busiest = jnp.max(jnp.where(away[None], tiles_used, 0))
        else:
            group, busiest = 0, capacity
        everyone = lax.dynamic_index_in_dim(everyone, group, 0, keepdims=False)
        live_tiles = lax.dynamic_index_in_dim(live_everywhere, group, 0, keepdims=False)
        partner_all = everyone[:, 0, :block_count]
        row_all = everyone[:, 1, :block_count]
        col_all = everyone[:, 2, :block_count]
        tile_range = jnp.arange(tile_count, dtype=jnp.int32)
        slot_range = jnp.arange(capacity, dtype=jnp.int32)
        mine = (
            (partner_all == me)
            & (row_all < live_tiles[:, None])
            & (col_all < live_tiles[me])
        )
        wants = jnp.any(mine[:, :, None] & (col_all[:, :, None] == tile_range), axis=1)
        want_place = jnp.cumsum(wants.astype(jnp.int32), axis=1) - 1
        hit = wants[:, :, None] & (want_place[:, :, None] == slot_range)
        wanted = jnp.sum(jnp.where(hit, tile_range[None, :, None], 0), axis=1)
        wanted = jnp.where(jnp.any(hit, axis=1), wanted, tile_count).reshape(slot_total)
        partner, row_tile, col_tile = partners[0, :, 0], row_tiles[0], col_tiles[0]
        partner_live = jnp.sum(
            jnp.where(partner[:, None] == part_range, live_tiles[None, :], 0), axis=1
        )
        alive = (row_tile < live_tiles[me]) & (col_tile < partner_live)
        same_partner = (partner[:, None] == partner[None, :]) & alive[None, :]
        same = same_partner & (col_tile[:, None] == col_tile[None, :])
        order = jnp.arange(block_count, dtype=jnp.int32)
        first = alive & ~jnp.any(same & (order[None, :] < order[:, None]), axis=1)
        lower = same_partner & first[None, :] & (col_tile[None, :] < col_tile[:, None])
        place = jnp.sum(lower.astype(jnp.int32), axis=1)
        slots = jnp.where(alive, partner * capacity + place, -1).astype(jnp.int32)
        firsts = first.astype(jnp.int32)

    tile_values = block_tiles[0]
    rep = lax.axis_index("rep")
    halves = [
        lax.dynamic_slice_in_dim(weight, half * columns, columns, 1) for half in (rep, 1 - rep)
    ]
    own_weight = jnp.concatenate(halves, axis=1)
    if near:
        with jax.named_scope("lists"):
            before = order[None, :] < order[:, None]
            after = order[None, :] > order[:, None]
            ahead = same_partner & (
                (col_tile[None, :] < col_tile[:, None])
                | ((col_tile[None, :] == col_tile[:, None]) & before)
            )
            rank = jnp.sum(ahead.astype(jnp.int32), axis=1)
            closing = alive & ~jnp.any(same & after, axis=1)
            slot_range = jnp.arange(slot_total, dtype=jnp.int32)
            ranked = alive[:, None] & ((partner * capacity + rank)[:, None] == slot_range)
            closed = closing[:, None] & (slots[:, None] == slot_range)

            def pick(hits, values, empty=0):
                return jnp.sum(jnp.where(hits, values[:, None] - empty, 0), axis=0) + empty

            same_row = alive[None, :] & (row_tile[:, None] == row_tile[None, :])
            sooner = alive[None, :] & (
                (row_tile[None, :] < row_tile[:, None])
                | ((row_tile[None, :] == row_tile[:, None]) & before)
            )
            row_rank = jnp.sum(sooner.astype(jnp.int32), axis=1)
            row_first = alive & ~jnp.any(same_row & before, axis=1)
            row_last = alive & ~jnp.any(same_row & after, axis=1)
            row_ranked = alive[:, None] & (row_rank[:, None] == order)
            row_closed = row_last[:, None] & (row_tile[:, None] == tile_range)
            lists = (
                live_counts,
                jnp.where(wanted < tile_count, wanted, 0),
                jnp.where(wants, want_place, -1).reshape(partitions * tile_count),
                pick(ranked, order),
                pick(ranked, row_tile),
                pick(ranked, 1 - firsts),
                pick(closed, rank),
                pick(row_ranked, order),
                pick(row_ranked, slots),
                pick(row_ranked, 1 - row_first.astype(jnp.int32)),
                pick(row_closed, row_rank, -1),
            )
        turns = turns_of(lax.axis_size("dom"), lax.axis_size("sub"))
        counts = list(range(max(1, capacity - 4), capacity + 1))
        branches = [
            functools.partial(
                whole,
                parts=partitions,
                turns=turns,
                capacity=capacity,
                count=count,
                identity=3 + i,
            )
            for i, count in enumerate(counts)
        ]
        chosen = jnp.clip(busiest - counts[0], 0, len(counts) - 1)
        return lax.switch(
            chosen, branches, *lists, state_pre, loss_grad, own_weight, tile_values
        )

    slot_shape = jax.ShapeDtypeStruct((slot_total, rows, columns), jnp.bfloat16)
    node_shape = jax.ShapeDtypeStruct((node_slots, columns), jnp.bfloat16)

    request, adjoint = pl.pallas_call(
        request_kernel,
        out_shape=(slot_shape, node_shape),
        in_specs=[smem(), smem(), vmem(), vmem()],
        out_specs=(vmem(), vmem()),
        scratch_shapes=[pltpu.VMEM((tile_count, rows, columns), jnp.bfloat16)],
        compiler_params=params(),
        name="request",
    )(live_counts, wanted, state_pre, loss_grad)
    received = trade_rows(request)
    gathered_sum = pl.pallas_call(
        gather_kernel,
        out_shape=node_shape,
        in_specs=[smem(), smem(), vmem(), vmem()],
        out_specs=vmem(),
        scratch_shapes=[pltpu.VMEM((tile_count, rows, columns), jnp.float32)],
        compiler_params=params(),
        name="gathered",
    )(slots, row_tile, received, tile_values)

    for iteration in range(ITERS):
        other = swap(adjoint)
        outgoing = pl.pallas_call(
            message_kernel,
            out_shape=slot_shape,
            in_specs=[smem(), smem(), smem(), vmem(), vmem(), vmem(), vmem()],
            out_specs=vmem(),
            scratch_shapes=[pltpu.VMEM((node_slots, columns), jnp.bfloat16)],
            compiler_params=params(),
            name="message",
        )(slots, firsts, row_tile, adjoint, other, own_weight, tile_values)
        incoming = trade_rows(outgoing)
        adjoint = pl.pallas_call(
            pull_kernel,
            out_shape=node_shape,
            in_specs=[smem(), smem(), vmem(), vmem(), vmem()],
            out_specs=vmem(),
            scratch_shapes=[pltpu.VMEM((tile_count, rows, columns), jnp.float32)],
            compiler_params=params(),
            name="pull",
        )(live_counts, wanted, incoming, state_pre, loss_grad)

    local_grad = lax.dot_general(
        gathered_sum,
        lax.all_gather(adjoint, "rep", axis=1, tiled=True),
        (((0,), (0,)), ((), ())),
        preferred_element_type=jnp.float32,
    )
    weight_grad = lax.psum(local_grad, PARTS) / math.sqrt(node_slots * partitions)
    return (adjoint, weight_grad)


def solution(mesh):
    return jax.shard_map(
        shards,
        mesh=mesh,
        in_specs=(
            P(("groups", "dom", "sub"), "rep"),
            P(("groups", "dom", "sub"), "rep"),
            P("rep", None),
            P(("groups", "dom", "sub")),
            P(("groups", "dom", "sub"), None, None),
            P(("groups", "dom", "sub"), None),
            P(("groups", "dom", "sub"), None),
            P(("groups", "dom", "sub"), None, None, None),
        ),
        out_specs=(P(("groups", "dom", "sub"), "rep"), P(("groups", "rep"), None)),
        check_vma=False,
    )
```

```python
import functools
import math

import jax
import jax.numpy as jnp
from jax import lax
from jax.experimental import pallas as pl
from jax.experimental.pallas import tpu as pltpu
from jax.sharding import PartitionSpec as P

ITERS = 3
VMEM_LIMIT = 48 * 1024 * 1024
PARTS = ("dom", "sub")
MESH = pl.DeviceIdType.MESH


def trade_rows(buffer):
    return lax.all_to_all(buffer, PARTS, split_axis=0, concat_axis=0, tiled=True)


def vmem():
    return pl.BlockSpec(memory_space=pltpu.VMEM)


def smem():
    return pl.BlockSpec(memory_space=pltpu.SMEM)


def params():
    return pltpu.CompilerParams(vmem_limit_bytes=VMEM_LIMIT)


def tile_rows(index, rows):
    return pl.ds(pl.multiple_of(index * rows, rows), rows)


def request_kernel(live, wanted, state_ref, loss_ref, out_ref, grad_ref, features):
    rows = out_ref.shape[1]
    tiles = state_ref.shape[0] // rows

    @pl.loop(0, tiles)
    def _(t):
        at = tile_rows(t, rows)
        row = lax.broadcasted_iota(jnp.int32, (rows, 1), 0) + t * rows
        keep = (row < live[0]).astype(jnp.float32)
        features[t] = (keep * jnp.tanh(state_ref[at, :].astype(jnp.float32))).astype(jnp.bfloat16)
        grad_ref[at, :] = (keep * loss_ref[at, :].astype(jnp.float32)).astype(jnp.bfloat16)

    @pl.loop(0, out_ref.shape[0])
    def _(s):
        @pl.when(wanted[s] < tiles)
        def _():
            out_ref[s] = features[wanted[s]]


def message_kernel(
    slots, firsts, row_tiles, own_ref, other_ref, weight_ref, tiles_ref, out_ref, mixed
):
    rows, columns = out_ref.shape[1:]
    tiles = own_ref.shape[0] // rows
    step = 4 * rows

    @pl.loop(0, tiles // 4)
    def _(t):
        at = tile_rows(t, step)
        both = jnp.concatenate([own_ref[at, :], other_ref[at, :]], axis=1)
        mixed[at, :] = lax.dot_general(
            both, weight_ref[...], (((1,), (1,)), ((), ())), preferred_element_type=jnp.float32
        ).astype(jnp.bfloat16)

    @pl.loop(0, tiles_ref.shape[0])
    def _(k):
        @pl.when(slots[k] >= 0)
        def _():
            message = lax.dot_general(
                tiles_ref[k],
                mixed[tile_rows(row_tiles[k], rows), :],
                (((0,), (0,)), ((), ())),
                preferred_element_type=jnp.float32,
            )
            slot = slots[k]

            @pl.when(firsts[k] == 1)
            def _():
                out_ref[slot] = message.astype(jnp.bfloat16)

            @pl.when(firsts[k] == 0)
            def _():
                out_ref[slot] = (out_ref[slot].astype(jnp.float32) + message).astype(jnp.bfloat16)


def pull_kernel(live, wanted, in_ref, state_ref, loss_ref, grad_ref, pulled):
    rows = in_ref.shape[1]
    tiles = state_ref.shape[0] // rows
    pulled[...] = jnp.zeros_like(pulled)

    @pl.loop(0, in_ref.shape[0])
    def _(s):
        @pl.when(wanted[s] < tiles)
        def _():
            pulled[wanted[s]] += in_ref[s].astype(jnp.float32)

    @pl.loop(0, tiles)
    def _(t):
        at = tile_rows(t, rows)
        row = lax.broadcasted_iota(jnp.int32, (rows, 1), 0) + t * rows
        keep = (row < live[0]).astype(jnp.float32)
        slope = 1.0 - jnp.tanh(state_ref[at, :].astype(jnp.float32)) ** 2
        value = slope * pulled[t] + loss_ref[at, :].astype(jnp.float32)
        grad_ref[at, :] = (keep * value).astype(jnp.bfloat16)


def gather_kernel(slots, row_tiles, in_ref, tiles_ref, out_ref, summed):
    rows = in_ref.shape[1]
    tiles = out_ref.shape[0] // rows
    summed[...] = jnp.zeros_like(summed)

    @pl.loop(0, tiles_ref.shape[0])
    def _(k):
        @pl.when(slots[k] >= 0)
        def _():
            summed[row_tiles[k]] += jnp.dot(
                tiles_ref[k], in_ref[slots[k]], preferred_element_type=jnp.float32
            )

    @pl.loop(0, tiles)
    def _(t):
        out_ref[tile_rows(t, rows), :] = summed[t].astype(jnp.bfloat16)


def peer_of(number):
    sub = lax.axis_size("sub")
    return {"dom": number // sub, "sub": lax.rem(number, sub)}


def position():
    return lax.axis_index("dom") * lax.axis_size("sub") + lax.axis_index("sub")


def greet(devices):
    barrier = pltpu.get_barrier_semaphore()
    for device in devices:
        pl.semaphore_signal(barrier, inc=1, device_id=device, device_id_type=MESH)
    pl.semaphore_wait(barrier, len(devices))


def remote(src, dst, send_sem, recv_sem, device):
    return pltpu.make_async_remote_copy(
        src_ref=src,
        dst_ref=dst,
        send_sem=send_sem,
        recv_sem=recv_sem,
        device_id=device,
        device_id_type=MESH,
    )


def table_kernel(in_ref, out_ref, send_sem, recv_sem, own_sem):
    groups, parts = out_ref.shape[0], out_ref.shape[1]
    group, me = lax.axis_index("groups"), position()
    others = []
    for turn in range(1, groups * parts):
        place = lax.rem(group * parts + me + turn, groups * parts)
        device = {"groups": place // parts, **peer_of(lax.rem(place, parts))}
        others.append(device)
    greet(others)
    copies = [
        remote(in_ref, out_ref.at[group, me], send_sem.at[i], recv_sem.at[i], device)
        for i, device in enumerate(others)
    ]
    for copy in copies:
        copy.start()
    own = pltpu.make_async_copy(in_ref, out_ref.at[group, me], own_sem)
    own.start()
    own.wait()
    for copy in copies:
        copy.wait()


def table_gather(table, groups, parts):
    count = groups * parts - 1
    return pl.pallas_call(
        table_kernel,
        out_shape=jax.ShapeDtypeStruct((groups, parts) + table.shape, table.dtype),
        in_specs=[vmem()],
        out_specs=vmem(),
        scratch_shapes=[
            pltpu.SemaphoreType.DMA((count,)),
            pltpu.SemaphoreType.DMA((count,)),
            pltpu.SemaphoreType.DMA,
        ],
        compiler_params=pltpu.CompilerParams(collective_id=0, has_side_effects=True),
        name="tables",
    )(table)


def turns_of(dom, sub):
    ahead = sorted(range(dom), key=lambda turn: -min(turn, dom - turn))
    return [(dz, dx) for dz in ahead for dx in range(sub) if dz or dx]


def whole_kernel(
    count, capacity, scale, turns, live, want_tile, in_place, block_at, row_at, same_at, last_at,
    sum_block, sum_slot, sum_same, sum_last, state_ref, loss_ref, weight_ref, tiles_any,
    grad_ref, total_ref,
    tiles, turned, features, slope, other, mixed, segment, outgoing, incoming_even, incoming_odd, request,
    arrived,
    running, summed, local, terms, share, parted,
    tile_sem, swap_send, swap_recv, send_sem, recv_sem, ask_send, ask_recv, sum_send, sum_recv,
    part_send, part_recv,
):
    blocks, rows, columns = tiles.shape
    nodes = state_ref.shape[0]
    tile_count = nodes // rows
    dom, sub = lax.axis_size("dom"), lax.axis_size("sub")
    parts = dom * sub
    z, x, rep = lax.axis_index("dom"), lax.axis_index("sub"), lax.axis_index("rep")
    me = z * sub + x
    peers, targets = [], []
    for dz, dx in turns:
        far = {"dom": lax.rem(z + dz, dom), "sub": lax.rem(x + dx, sub)}
        peers.append(far)
        targets.append(far["dom"] * sub + far["sub"])
    core = {"rep": 1 - rep}
    fetch = pltpu.make_async_copy(tiles_any, tiles, tile_sem)
    fetch.start()
    greet(peers + [core])
    quarters = 4
    incoming = (incoming_even, incoming_odd)
    quarter = nodes // quarters

    def swap_copy(turn, part):
        at = pl.ds(part * quarter, quarter)
        return remote(
            grad_ref.at[at],
            other.at[turn % 2, at],
            swap_send.at[turn, part],
            swap_recv.at[turn, part],
            core,
        )

    def keep_of(t):
        row = lax.broadcasted_iota(jnp.int32, (rows, 1), 0) + t * rows
        return (row < live[0]).astype(jnp.float32)

    for part in range(quarters):

        @pl.loop(part * tile_count // quarters, (part + 1) * tile_count // quarters)
        def _(t):
            at = tile_rows(t, rows)
            grad_ref[at, :] = (keep_of(t) * loss_ref[at, :].astype(jnp.float32)).astype(
                jnp.bfloat16
            )

        swap_copy(0, part).start()

    @pl.loop(0, tile_count)
    def _(t):
        at = tile_rows(t, rows)
        value = jnp.tanh(state_ref[at, :].astype(jnp.float32))
        features[t] = (keep_of(t) * value).astype(jnp.bfloat16)
        slope[t] = 1.0 - value * value

    def act_on(i, copy, act, sending):
        dz, sign = turns[i][0], 1 if sending else -1
        if count == capacity or dz == 0:
            act(copy(i, capacity))
        elif 2 * dz == dom:
            act(copy(i, count))
        else:
            there = lax.rem(z + sign * dz + dom, dom)
            crossing = (2 * z) // dom != (2 * there) // dom

            @pl.when(crossing)
            def _():
                act(copy(i, count))

            @pl.when(jnp.logical_not(crossing))
            def _():
                act(copy(i, capacity))

    def start(i, copy):
        act_on(i, copy, lambda it: it.start(), True)

    def finish(i, copy):
        act_on(i, copy, lambda it: it.wait_send(), True)
        act_on(i, copy, lambda it: it.wait_recv(), False)

    def ask_copy(i, size):
        return remote(
            request.at[targets[i], pl.ds(0, size)],
            arrived.at[me, pl.ds(0, size)],
            ask_send.at[i],
            ask_recv.at[i],
            peers[i],
        )

    def ask(i):
        @pl.loop(0, capacity)
        def _(s):
            request[targets[i], s] = features[want_tile[targets[i] * capacity + s]]

        start(i, ask_copy)

    many = len(turns)
    early, later = 2 * many // 7, 5 * many // 7
    for i in range(early):
        ask(i)

    fetch.wait()

    @pl.loop(0, blocks, unroll=2)
    def _(k):
        turned[k] = tiles[k].T

    def messages_to(target, into):
        def add(j, total):
            at = target * capacity + j
            message = jnp.dot(
                turned[block_at[at]], mixed[row_at[at]], preferred_element_type=jnp.float32
            )
            total = jnp.where(same_at[at] > 0, total, 0.0) + message
            segment[j] = total.astype(jnp.bfloat16)
            return total

        lax.fori_loop(0, capacity, add, jnp.zeros((rows, columns), jnp.float32), unroll=4)

        @pl.loop(0, capacity)
        def _(s):
            into[target, s] = segment[last_at[target * capacity + s]]

    def send_copy(turn, i, size):
        return remote(
            outgoing.at[targets[i], pl.ds(0, size)],
            incoming[turn % 2].at[me, pl.ds(0, size)],
            send_sem.at[turn, i],
            recv_sem.at[turn, i],
            peers[i],
        )

    for turn in range(ITERS):
        step = quarter // rows
        for part in range(quarters):
            swap_copy(turn, part).wait()

            @pl.loop(part * step // 4, (part + 1) * step // 4)
            def _(t):
                at = tile_rows(t, 4 * rows)
                both = jnp.concatenate([grad_ref[at, :], other[turn % 2, at, :]], axis=1)
                product = lax.dot_general(
                    both,
                    weight_ref[...],
                    (((1,), (1,)), ((), ())),
                    preferred_element_type=jnp.float32,
                )
                mixed[pl.ds(4 * t, 4)] = product.astype(jnp.bfloat16).reshape(4, rows, columns)

        for i in range(many):
            messages_to(targets[i], outgoing)
            start(i, functools.partial(send_copy, turn))
        messages_to(me, incoming[turn % 2])
        if turn == 0:
            for i in range(early, later):
                ask(i)
        elif turn == 1:
            for i in range(later, many):
                ask(i)

            @pl.loop(0, capacity)
            def _(s):
                arrived[me, s] = features[want_tile[me * capacity + s]]

        else:
            for i in range(many):
                finish(i, ask_copy)

            def add(j, total):
                slot = sum_slot[j]
                product = jnp.dot(
                    tiles[sum_block[j]],
                    arrived[slot // capacity, lax.rem(slot, capacity)],
                    preferred_element_type=jnp.float32,
                )
                total = jnp.where(sum_same[j] > 0, total, 0.0) + product
                running[j] = total
                return total

            lax.fori_loop(0, blocks, add, jnp.zeros((rows, columns), jnp.float32), unroll=4)

            @pl.loop(0, tile_count)
            def _(t):
                last = sum_last[t]
                value = jnp.where(last >= 0, running[jnp.maximum(last, 0)], 0.0)
                summed[tile_rows(t, rows), :] = value.astype(jnp.bfloat16)

        for i in range(many):
            finish(i, functools.partial(send_copy, turn))
        for part in range(quarters):

            @pl.loop(part * step, (part + 1) * step, unroll=2)
            def _(t):
                at = tile_rows(t, rows)
                total = jnp.zeros((rows, columns), jnp.float32)
                for source in range(parts):
                    place = in_place[source * tile_count + t]
                    value = incoming[turn % 2][source, jnp.maximum(place, 0)]
                    total = total + jnp.where(place >= 0, value.astype(jnp.float32), 0.0)
                value = slope[t] * total + loss_ref[at, :].astype(jnp.float32)
                grad_ref[at, :] = (keep_of(t) * value).astype(jnp.bfloat16)

            swap_copy(turn + 1, part).start()

    local[rep] = columns_product(summed, grad_ref)
    for part in range(quarters):
        swap_copy(ITERS, part).wait()
    local[1 - rep] = columns_product(summed, other.at[ITERS % 2])
    share_rows = columns // parts

    def rows_of(number):
        return pl.ds(pl.multiple_of(number * share_rows, share_rows), share_rows)

    copies = [
        remote(
            local.at[:, rows_of(target), :], terms.at[me], sum_send.at[i], sum_recv.at[i], peer
        )
        for i, (target, peer) in enumerate(zip(targets, peers))
    ]
    for copy in copies:
        copy.start()
    terms[me] = local[:, rows_of(me), :]
    for copy in copies:
        copy.wait()
    share[...] = jnp.sum(terms[...], axis=0) * scale
    copies = [
        remote(share, parted.at[me], part_send.at[i], part_recv.at[i], peer)
        for i, peer in enumerate(peers)
    ]
    for copy in copies:
        copy.start()
    parted[me] = share[...]
    for copy in copies:
        copy.wait()
    for part in range(parts):
        for side in range(2):
            total_ref[
                part * share_rows : (part + 1) * share_rows, side * columns : (side + 1) * columns
            ] = parted[part, side]


def whole(*operands, parts, turns, capacity, count, identity):
    state_pre, tile_values = operands[-4], operands[-1]
    nodes, columns = state_pre.shape
    blocks, rows, _ = tile_values.shape
    tile_count = nodes // rows
    many = len(turns)
    slots = (parts, capacity, rows, columns)
    dma = pltpu.SemaphoreType.DMA
    return pl.pallas_call(
        functools.partial(
            whole_kernel, count, capacity, 1.0 / math.sqrt(nodes * parts), turns
        ),
        out_shape=(
            jax.ShapeDtypeStruct((nodes, columns), jnp.bfloat16),
            jax.ShapeDtypeStruct((columns, 2 * columns), jnp.float32),
        ),
        in_specs=[smem()] * (len(operands) - 4)
        + [vmem()] * 3
        + [pl.BlockSpec(memory_space=pl.ANY)],
        out_specs=(vmem(), vmem()),
        scratch_shapes=[
            pltpu.VMEM((blocks, rows, rows), jnp.bfloat16),
            pltpu.VMEM((blocks, rows, rows), jnp.bfloat16),
            pltpu.VMEM((tile_count, rows, columns), jnp.bfloat16),
            pltpu.VMEM((tile_count, rows, columns), jnp.float32),
            pltpu.VMEM((2, nodes, columns), jnp.bfloat16),
            pltpu.VMEM((tile_count, rows, columns), jnp.bfloat16),
            pltpu.VMEM((capacity, rows, columns), jnp.bfloat16),
            pltpu.VMEM(slots, jnp.bfloat16),
            pltpu.VMEM(slots, jnp.bfloat16),
            pltpu.VMEM(slots, jnp.bfloat16),
            pltpu.VMEM(slots, jnp.bfloat16),
            pltpu.VMEM(slots, jnp.bfloat16),
            pltpu.VMEM((blocks, rows, columns), jnp.float32),
            pltpu.VMEM((nodes, columns), jnp.bfloat16),
            pltpu.VMEM((2, columns, columns), jnp.float32),
            pltpu.VMEM((parts, 2, columns // parts, columns), jnp.float32),
            pltpu.VMEM((2, columns // parts, columns), jnp.float32),
            pltpu.VMEM((parts, 2, columns // parts, columns), jnp.float32),
            dma,
            dma((ITERS + 1, 4)),
            dma((ITERS + 1, 4)),
            dma((ITERS, many)),
            dma((ITERS, many)),
            dma((many,)),
            dma((many,)),
            dma((many,)),
            dma((many,)),
            dma((many,)),
            dma((many,)),
        ],
        compiler_params=pltpu.CompilerParams(
            collective_id=identity, has_side_effects=True, vmem_limit_bytes=60 * 1024 * 1024
        ),
        name="whole",
    )(*operands)


def swap_kernel(in_ref, out_ref, send_sem, recv_sem):
    other = {"rep": 1 - lax.axis_index("rep")}
    greet([other])
    copy = remote(in_ref, out_ref, send_sem, recv_sem, other)
    copy.start()
    copy.wait()


def swap(array):
    return pl.pallas_call(
        swap_kernel,
        out_shape=jax.ShapeDtypeStruct(array.shape, array.dtype),
        in_specs=[pl.BlockSpec(memory_space=pl.ANY)],
        out_specs=pl.BlockSpec(memory_space=pl.ANY),
        scratch_shapes=[pltpu.SemaphoreType.DMA, pltpu.SemaphoreType.DMA],
        compiler_params=pltpu.CompilerParams(collective_id=1, has_side_effects=True),
        name="swap",
    )(array)


def columns_product(sum_ref, grad_ref):
    nodes = sum_ref.shape[0]
    step = 1024 if nodes % 1024 == 0 else nodes

    def add(t, total):
        at = tile_rows(t, step)
        return total + lax.dot_general(
            sum_ref[at, :], grad_ref[at, :], (((0,), (0,)), ((), ())),
            preferred_element_type=jnp.float32,
        )

    zero = jnp.zeros((sum_ref.shape[1], grad_ref.shape[1]), jnp.float32)
    return lax.fori_loop(0, nodes // step, add, zero)


def shards(state_pre, loss_grad, weight, live_counts, partners, row_tiles, col_tiles, block_tiles):
    node_slots, columns = state_pre.shape
    partitions = lax.axis_size("dom") * lax.axis_size("sub")
    groups = lax.axis_size("groups")
    me = position()
    near = partitions <= 16 and columns % (8 * partitions) == 0
    block_count = row_tiles.shape[1]
    rows = block_tiles.shape[2]
    tile_count = node_slots // rows
    capacity = max(2, 4 * block_count // (3 * partitions))
    slot_total = partitions * capacity

    with jax.named_scope("tables"):
        table = jnp.stack(
            [
                jnp.pad(row, (0, -row.shape[0] % 128))
                for row in (
                    partners[0, :, 0],
                    row_tiles[0],
                    col_tiles[0],
                    jnp.broadcast_to(live_counts, (block_count,)),
                )
            ]
        )
        table = jnp.pad(table, ((0, 4), (0, 0)))
        if near:
            everyone = table_gather(table, groups, partitions)
        else:
            everyone = lax.all_gather(table, PARTS)[None]
        live_everywhere = (everyone[:, :, 3, 0] + rows - 1) // rows
        part_range = jnp.arange(partitions, dtype=jnp.int32)
        if near:
            group = lax.axis_index("groups")
            partner_each = everyone[:, :, 0, :block_count, None] == part_range
            partner_live = jnp.sum(
                jnp.where(partner_each, live_everywhere[:, None, None, :], 0), axis=3
            )
            alive_each = (everyone[:, :, 1, :block_count] < live_everywhere[:, :, None]) & (
                everyone[:, :, 2, :block_count] < partner_live
            )
            col_each = everyone[:, :, 2, :block_count, None] == jnp.arange(tile_count)
            used = jnp.einsum(
                "gpkq,gpkt->gpqt",
                (partner_each & alive_each[..., None]).astype(jnp.bfloat16),
                col_each.astype(jnp.bfloat16),
                preferred_element_type=jnp.float32,
            )
            side = 2 * (part_range // lax.axis_size("sub")) // lax.axis_size("dom")
            away = side[:, None] != side[None, :]
            tiles_used = jnp.sum((used > 0).astype(jnp.int32), axis=3)
            busiest = jnp.max(jnp.where(away[None], tiles_used, 0))
        else:
            group, busiest = 0, capacity
        everyone = lax.dynamic_index_in_dim(everyone, group, 0, keepdims=False)
        live_tiles = lax.dynamic_index_in_dim(live_everywhere, group, 0, keepdims=False)
        partner_all = everyone[:, 0, :block_count]
        row_all = everyone[:, 1, :block_count]
        col_all = everyone[:, 2, :block_count]
        tile_range = jnp.arange(tile_count, dtype=jnp.int32)
        slot_range = jnp.arange(capacity, dtype=jnp.int32)
        mine = (
            (partner_all == me)
            & (row_all < live_tiles[:, None])
            & (col_all < live_tiles[me])
        )
        wants = jnp.any(mine[:, :, None] & (col_all[:, :, None] == tile_range), axis=1)
        want_place = jnp.cumsum(wants.astype(jnp.int32), axis=1) - 1
        hit = wants[:, :, None] & (want_place[:, :, None] == slot_range)
        wanted = jnp.sum(jnp.where(hit, tile_range[None, :, None], 0), axis=1)
        wanted = jnp.where(jnp.any(hit, axis=1), wanted, tile_count).reshape(slot_total)
        partner, row_tile, col_tile = partners[0, :, 0], row_tiles[0], col_tiles[0]
        partner_live = jnp.sum(
            jnp.where(partner[:, None] == part_range, live_tiles[None, :], 0), axis=1
        )
        alive = (row_tile < live_tiles[me]) & (col_tile < partner_live)
        same_partner = (partner[:, None] == partner[None, :]) & alive[None, :]
        same = same_partner & (col_tile[:, None] == col_tile[None, :])
        order = jnp.arange(block_count, dtype=jnp.int32)
        first = alive & ~jnp.any(same & (order[None, :] < order[:, None]), axis=1)
        lower = same_partner & first[None, :] & (col_tile[None, :] < col_tile[:, None])
        place = jnp.sum(lower.astype(jnp.int32), axis=1)
        slots = jnp.where(alive, partner * capacity + place, -1).astype(jnp.int32)
        firsts = first.astype(jnp.int32)

    tile_values = block_tiles[0]
    rep = lax.axis_index("rep")
    halves = [
        lax.dynamic_slice_in_dim(weight, half * columns, columns, 1) for half in (rep, 1 - rep)
    ]
    own_weight = jnp.concatenate(halves, axis=1)
    if near:
        with jax.named_scope("lists"):
            before = order[None, :] < order[:, None]
            after = order[None, :] > order[:, None]
            ahead = same_partner & (
                (col_tile[None, :] < col_tile[:, None])
                | ((col_tile[None, :] == col_tile[:, None]) & before)
            )
            rank = jnp.sum(ahead.astype(jnp.int32), axis=1)
            closing = alive & ~jnp.any(same & after, axis=1)
            slot_range = jnp.arange(slot_total, dtype=jnp.int32)
            ranked = alive[:, None] & ((partner * capacity + rank)[:, None] == slot_range)
            closed = closing[:, None] & (slots[:, None] == slot_range)

            def pick(hits, values, empty=0):
                return jnp.sum(jnp.where(hits, values[:, None] - empty, 0), axis=0) + empty

            same_row = alive[None, :] & (row_tile[:, None] == row_tile[None, :])
            sooner = alive[None, :] & (
                (row_tile[None, :] < row_tile[:, None])
                | ((row_tile[None, :] == row_tile[:, None]) & before)
            )
            row_rank = jnp.sum(sooner.astype(jnp.int32), axis=1)
            row_first = alive & ~jnp.any(same_row & before, axis=1)
            row_last = alive & ~jnp.any(same_row & after, axis=1)
            row_ranked = alive[:, None] & (row_rank[:, None] == order)
            row_closed = row_last[:, None] & (row_tile[:, None] == tile_range)
            lists = (
                live_counts,
                jnp.where(wanted < tile_count, wanted, 0),
                jnp.where(wants, want_place, -1).reshape(partitions * tile_count),
                pick(ranked, order),
                pick(ranked, row_tile),
                pick(ranked, 1 - firsts),
                pick(closed, rank),
                pick(row_ranked, order),
                pick(row_ranked, slots),
                pick(row_ranked, 1 - row_first.astype(jnp.int32)),
                pick(row_closed, row_rank, -1),
            )
        turns = turns_of(lax.axis_size("dom"), lax.axis_size("sub"))
        counts = list(range(max(1, capacity - 4), capacity + 1))
        branches = [
            functools.partial(
                whole,
                parts=partitions,
                turns=turns,
                capacity=capacity,
                count=count,
                identity=3 + i,
            )
            for i, count in enumerate(counts)
        ]
        chosen = jnp.clip(busiest - counts[0], 0, len(counts) - 1)
        return lax.switch(
            chosen, branches, *lists, state_pre, loss_grad, own_weight, tile_values
        )

    slot_shape = jax.ShapeDtypeStruct((slot_total, rows, columns), jnp.bfloat16)
    node_shape = jax.ShapeDtypeStruct((node_slots, columns), jnp.bfloat16)

    request, adjoint = pl.pallas_call(
        request_kernel,
        out_shape=(slot_shape, node_shape),
        in_specs=[smem(), smem(), vmem(), vmem()],
        out_specs=(vmem(), vmem()),
        scratch_shapes=[pltpu.VMEM((tile_count, rows, columns), jnp.bfloat16)],
        compiler_params=params(),
        name="request",
    )(live_counts, wanted, state_pre, loss_grad)
    received = trade_rows(request)
    gathered_sum = pl.pallas_call(
        gather_kernel,
        out_shape=node_shape,
        in_specs=[smem(), smem(), vmem(), vmem()],
        out_specs=vmem(),
        scratch_shapes=[pltpu.VMEM((tile_count, rows, columns), jnp.float32)],
        compiler_params=params(),
        name="gathered",
    )(slots, row_tile, received, tile_values)

    for iteration in range(ITERS):
        other = swap(adjoint)
        outgoing = pl.pallas_call(
            message_kernel,
            out_shape=slot_shape,
            in_specs=[smem(), smem(), smem(), vmem(), vmem(), vmem(), vmem()],
            out_specs=vmem(),
            scratch_shapes=[pltpu.VMEM((node_slots, columns), jnp.bfloat16)],
            compiler_params=params(),
            name="message",
        )(slots, firsts, row_tile, adjoint, other, own_weight, tile_values)
        incoming = trade_rows(outgoing)
        adjoint = pl.pallas_call(
            pull_kernel,
            out_shape=node_shape,
            in_specs=[smem(), smem(), vmem(), vmem(), vmem()],
            out_specs=vmem(),
            scratch_shapes=[pltpu.VMEM((tile_count, rows, columns), jnp.float32)],
            compiler_params=params(),
            name="pull",
        )(live_counts, wanted, incoming, state_pre, loss_grad)

    local_grad = lax.dot_general(
        gathered_sum,
        lax.all_gather(adjoint, "rep", axis=1, tiled=True),
        (((0,), (0,)), ((), ())),
        preferred_element_type=jnp.float32,
    )
    weight_grad = lax.psum(local_grad, PARTS) / math.sqrt(node_slots * partitions)
    return (adjoint, weight_grad)


def solution(mesh):
    return jax.shard_map(
        shards,
        mesh=mesh,
        in_specs=(
            P(("groups", "dom", "sub"), "rep"),
            P(("groups", "dom", "sub"), "rep"),
            P("rep", None),
            P(("groups", "dom", "sub")),
            P(("groups", "dom", "sub"), None, None),
            P(("groups", "dom", "sub"), None),
            P(("groups", "dom", "sub"), None),
            P(("groups", "dom", "sub"), None, None, None),
        ),
        out_specs=(P(("groups", "dom", "sub"), "rep"), P(("groups", "rep"), None)),
        check_vma=False,
    )
```

```python
import functools
import math

import jax
import jax.numpy as jnp
from jax import lax
from jax.experimental import pallas as pl
from jax.experimental.pallas import tpu as pltpu
from jax.sharding import PartitionSpec as P

ITERS = 3
VMEM_LIMIT = 48 * 1024 * 1024
PARTS = ("dom", "sub")
MESH = pl.DeviceIdType.MESH


def trade_rows(buffer):
    return lax.all_to_all(buffer, PARTS, split_axis=0, concat_axis=0, tiled=True)


def vmem():
    return pl.BlockSpec(memory_space=pltpu.VMEM)


def smem():
    return pl.BlockSpec(memory_space=pltpu.SMEM)


def params():
    return pltpu.CompilerParams(vmem_limit_bytes=VMEM_LIMIT)


def tile_rows(index, rows):
    return pl.ds(pl.multiple_of(index * rows, rows), rows)


def request_kernel(live, wanted, state_ref, loss_ref, out_ref, grad_ref, features):
    rows = out_ref.shape[1]
    tiles = state_ref.shape[0] // rows

    @pl.loop(0, tiles)
    def _(t):
        at = tile_rows(t, rows)
        row = lax.broadcasted_iota(jnp.int32, (rows, 1), 0) + t * rows
        keep = (row < live[0]).astype(jnp.float32)
        features[t] = (keep * jnp.tanh(state_ref[at, :].astype(jnp.float32))).astype(jnp.bfloat16)
        grad_ref[at, :] = (keep * loss_ref[at, :].astype(jnp.float32)).astype(jnp.bfloat16)

    @pl.loop(0, out_ref.shape[0])
    def _(s):
        @pl.when(wanted[s] < tiles)
        def _():
            out_ref[s] = features[wanted[s]]


def message_kernel(
    slots, firsts, row_tiles, own_ref, other_ref, weight_ref, tiles_ref, out_ref, mixed
):
    rows, columns = out_ref.shape[1:]
    tiles = own_ref.shape[0] // rows
    step = 4 * rows

    @pl.loop(0, tiles // 4)
    def _(t):
        at = tile_rows(t, step)
        both = jnp.concatenate([own_ref[at, :], other_ref[at, :]], axis=1)
        mixed[at, :] = lax.dot_general(
            both, weight_ref[...], (((1,), (1,)), ((), ())), preferred_element_type=jnp.float32
        ).astype(jnp.bfloat16)

    @pl.loop(0, tiles_ref.shape[0])
    def _(k):
        @pl.when(slots[k] >= 0)
        def _():
            message = lax.dot_general(
                tiles_ref[k],
                mixed[tile_rows(row_tiles[k], rows), :],
                (((0,), (0,)), ((), ())),
                preferred_element_type=jnp.float32,
            )
            slot = slots[k]

            @pl.when(firsts[k] == 1)
            def _():
                out_ref[slot] = message.astype(jnp.bfloat16)

            @pl.when(firsts[k] == 0)
            def _():
                out_ref[slot] = (out_ref[slot].astype(jnp.float32) + message).astype(jnp.bfloat16)


def pull_kernel(live, wanted, in_ref, state_ref, loss_ref, grad_ref, pulled):
    rows = in_ref.shape[1]
    tiles = state_ref.shape[0] // rows
    pulled[...] = jnp.zeros_like(pulled)

    @pl.loop(0, in_ref.shape[0])
    def _(s):
        @pl.when(wanted[s] < tiles)
        def _():
            pulled[wanted[s]] += in_ref[s].astype(jnp.float32)

    @pl.loop(0, tiles)
    def _(t):
        at = tile_rows(t, rows)
        row = lax.broadcasted_iota(jnp.int32, (rows, 1), 0) + t * rows
        keep = (row < live[0]).astype(jnp.float32)
        slope = 1.0 - jnp.tanh(state_ref[at, :].astype(jnp.float32)) ** 2
        value = slope * pulled[t] + loss_ref[at, :].astype(jnp.float32)
        grad_ref[at, :] = (keep * value).astype(jnp.bfloat16)


def gather_kernel(slots, row_tiles, in_ref, tiles_ref, out_ref, summed):
    rows = in_ref.shape[1]
    tiles = out_ref.shape[0] // rows
    summed[...] = jnp.zeros_like(summed)

    @pl.loop(0, tiles_ref.shape[0])
    def _(k):
        @pl.when(slots[k] >= 0)
        def _():
            summed[row_tiles[k]] += jnp.dot(
                tiles_ref[k], in_ref[slots[k]], preferred_element_type=jnp.float32
            )

    @pl.loop(0, tiles)
    def _(t):
        out_ref[tile_rows(t, rows), :] = summed[t].astype(jnp.bfloat16)


def peer_of(number):
    sub = lax.axis_size("sub")
    return {"dom": number // sub, "sub": lax.rem(number, sub)}


def position():
    return lax.axis_index("dom") * lax.axis_size("sub") + lax.axis_index("sub")


def greet(devices):
    barrier = pltpu.get_barrier_semaphore()
    for device in devices:
        pl.semaphore_signal(barrier, inc=1, device_id=device, device_id_type=MESH)
    pl.semaphore_wait(barrier, len(devices))


def remote(src, dst, send_sem, recv_sem, device):
    return pltpu.make_async_remote_copy(
        src_ref=src,
        dst_ref=dst,
        send_sem=send_sem,
        recv_sem=recv_sem,
        device_id=device,
        device_id_type=MESH,
    )


def table_kernel(in_ref, out_ref, send_sem, recv_sem, own_sem):
    groups, parts = out_ref.shape[0], out_ref.shape[1]
    group, me = lax.axis_index("groups"), position()
    others = []
    for turn in range(1, groups * parts):
        place = lax.rem(group * parts + me + turn, groups * parts)
        device = {"groups": place // parts, **peer_of(lax.rem(place, parts))}
        others.append(device)
    greet(others)
    copies = [
        remote(in_ref, out_ref.at[group, me], send_sem.at[i], recv_sem.at[i], device)
        for i, device in enumerate(others)
    ]
    for copy in copies:
        copy.start()
    own = pltpu.make_async_copy(in_ref, out_ref.at[group, me], own_sem)
    own.start()
    own.wait()
    for copy in copies:
        copy.wait()


def table_gather(table, groups, parts):
    count = groups * parts - 1
    return pl.pallas_call(
        table_kernel,
        out_shape=jax.ShapeDtypeStruct((groups, parts) + table.shape, table.dtype),
        in_specs=[vmem()],
        out_specs=vmem(),
        scratch_shapes=[
            pltpu.SemaphoreType.DMA((count,)),
            pltpu.SemaphoreType.DMA((count,)),
            pltpu.SemaphoreType.DMA,
        ],
        compiler_params=pltpu.CompilerParams(collective_id=0, has_side_effects=True),
        name="tables",
    )(table)


def turns_of(dom, sub):
    ahead = sorted(range(dom), key=lambda turn: -min(turn, dom - turn))
    return [(dz, dx) for dz in ahead for dx in range(sub) if dz or dx]


def whole_kernel(
    count, capacity, scale, turns, live, want_tile, in_place, block_at, row_at, same_at, last_at,
    sum_block, sum_slot, sum_same, sum_last, state_ref, loss_ref, weight_ref, tiles_any,
    grad_ref, total_ref,
    tiles, turned, features, slope, other, mixed, segment, outgoing, incoming_even, incoming_odd, request,
    arrived,
    running, summed, local, terms, share, parted,
    tile_sem, swap_send, swap_recv, send_sem, recv_sem, ask_send, ask_recv, sum_send, sum_recv,
    part_send, part_recv,
):
    blocks, rows, columns = tiles.shape
    nodes = state_ref.shape[0]
    tile_count = nodes // rows
    dom, sub = lax.axis_size("dom"), lax.axis_size("sub")
    parts = dom * sub
    z, x, rep = lax.axis_index("dom"), lax.axis_index("sub"), lax.axis_index("rep")
    me = z * sub + x
    peers, targets = [], []
    for dz, dx in turns:
        far = {"dom": lax.rem(z + dz, dom), "sub": lax.rem(x + dx, sub)}
        peers.append(far)
        targets.append(far["dom"] * sub + far["sub"])
    core = {"rep": 1 - rep}
    fetch = pltpu.make_async_copy(tiles_any, tiles, tile_sem)
    fetch.start()
    greet(peers + [core])
    quarters = 4
    incoming = (incoming_even, incoming_odd)
    quarter = nodes // quarters

    def swap_copy(turn, part):
        at = pl.ds(part * quarter, quarter)
        return remote(
            grad_ref.at[at],
            other.at[turn % 2, at],
            swap_send.at[turn, part],
            swap_recv.at[turn, part],
            core,
        )

    def keep_of(t):
        row = lax.broadcasted_iota(jnp.int32, (rows, 1), 0) + t * rows
        return (row < live[0]).astype(jnp.float32)

    for part in range(quarters):

        @pl.loop(part * tile_count // quarters, (part + 1) * tile_count // quarters)
        def _(t):
            at = tile_rows(t, rows)
            grad_ref[at, :] = (keep_of(t) * loss_ref[at, :].astype(jnp.float32)).astype(
                jnp.bfloat16
            )

        swap_copy(0, part).start()

    @pl.loop(0, tile_count)
    def _(t):
        at = tile_rows(t, rows)
        value = jnp.tanh(state_ref[at, :].astype(jnp.float32))
        features[t] = (keep_of(t) * value).astype(jnp.bfloat16)
        slope[t] = 1.0 - value * value

    fetch.wait()

    @pl.loop(0, blocks, unroll=2)
    def _(k):
        turned[k] = tiles[k].T

    def ask(i):
        target = targets[i]

        @pl.loop(0, count)
        def _(s):
            request[target, s] = features[want_tile[target * capacity + s]]

        remote(
            request.at[target, pl.ds(0, count)],
            arrived.at[me, pl.ds(0, count)],
            ask_send.at[i],
            ask_recv.at[i],
            peers[i],
        ).start()

    def ask_copy(i):
        return remote(
            request.at[targets[i], pl.ds(0, count)],
            arrived.at[me, pl.ds(0, count)],
            ask_send.at[i],
            ask_recv.at[i],
            peers[i],
        )

    def messages_to(target, into):
        def add(j, total):
            at = target * capacity + j
            message = jnp.dot(
                turned[block_at[at]], mixed[row_at[at]], preferred_element_type=jnp.float32
            )
            total = jnp.where(same_at[at] > 0, total, 0.0) + message
            segment[j] = total.astype(jnp.bfloat16)
            return total

        lax.fori_loop(0, capacity, add, jnp.zeros((rows, columns), jnp.float32), unroll=4)

        @pl.loop(0, count if into is outgoing else capacity)
        def _(s):
            into[target, s] = segment[last_at[target * capacity + s]]

    def send_copy(turn, i):
        return remote(
            outgoing.at[targets[i], pl.ds(0, count)],
            incoming[turn % 2].at[me, pl.ds(0, count)],
            send_sem.at[turn, i],
            recv_sem.at[turn, i],
            peers[i],
        )

    many = len(turns)
    half = (many + 1) // 2
    for turn in range(ITERS):
        step = quarter // rows
        for part in range(quarters):
            swap_copy(turn, part).wait()

            @pl.loop(part * step // 4, (part + 1) * step // 4)
            def _(t):
                at = tile_rows(t, 4 * rows)
                both = jnp.concatenate([grad_ref[at, :], other[turn % 2, at, :]], axis=1)
                product = lax.dot_general(
                    both,
                    weight_ref[...],
                    (((1,), (1,)), ((), ())),
                    preferred_element_type=jnp.float32,
                )
                mixed[pl.ds(4 * t, 4)] = product.astype(jnp.bfloat16).reshape(4, rows, columns)

        for i in range(many):
            messages_to(targets[i], outgoing)
            send_copy(turn, i).start()
        messages_to(me, incoming[turn % 2])
        if turn == 0:
            for i in range(half):
                ask(i)
        elif turn == 1:
            for i in range(half, many):
                ask(i)

            @pl.loop(0, capacity)
            def _(s):
                arrived[me, s] = features[want_tile[me * capacity + s]]

        else:
            for i in range(many):
                ask_copy(i).wait()

            def add(j, total):
                slot = sum_slot[j]
                product = jnp.dot(
                    tiles[sum_block[j]],
                    arrived[slot // capacity, lax.rem(slot, capacity)],
                    preferred_element_type=jnp.float32,
                )
                total = jnp.where(sum_same[j] > 0, total, 0.0) + product
                running[j] = total
                return total

            lax.fori_loop(0, blocks, add, jnp.zeros((rows, columns), jnp.float32), unroll=4)

            @pl.loop(0, tile_count)
            def _(t):
                last = sum_last[t]
                value = jnp.where(last >= 0, running[jnp.maximum(last, 0)], 0.0)
                summed[tile_rows(t, rows), :] = value.astype(jnp.bfloat16)

        for i in range(many):
            send_copy(turn, i).wait()
        for part in range(quarters):

            @pl.loop(part * step, (part + 1) * step)
            def _(t):
                at = tile_rows(t, rows)
                total = jnp.zeros((rows, columns), jnp.float32)
                for source in range(parts):
                    place = in_place[source * tile_count + t]
                    value = incoming[turn % 2][source, jnp.maximum(place, 0)]
                    total = total + jnp.where(place >= 0, value.astype(jnp.float32), 0.0)
                value = slope[t] * total + loss_ref[at, :].astype(jnp.float32)
                grad_ref[at, :] = (keep_of(t) * value).astype(jnp.bfloat16)

            swap_copy(turn + 1, part).start()

    local[rep] = columns_product(summed, grad_ref)
    for part in range(quarters):
        swap_copy(ITERS, part).wait()
    local[1 - rep] = columns_product(summed, other.at[ITERS % 2])
    share_rows = columns // parts

    def rows_of(number):
        return pl.ds(pl.multiple_of(number * share_rows, share_rows), share_rows)

    copies = [
        remote(
            local.at[:, rows_of(target), :], terms.at[me], sum_send.at[i], sum_recv.at[i], peer
        )
        for i, (target, peer) in enumerate(zip(targets, peers))
    ]
    for copy in copies:
        copy.start()
    terms[me] = local[:, rows_of(me), :]
    for copy in copies:
        copy.wait()
    share[...] = jnp.sum(terms[...], axis=0) * scale
    copies = [
        remote(share, parted.at[me], part_send.at[i], part_recv.at[i], peer)
        for i, peer in enumerate(peers)
    ]
    for copy in copies:
        copy.start()
    parted[me] = share[...]
    for copy in copies:
        copy.wait()
    for part in range(parts):
        for side in range(2):
            total_ref[
                part * share_rows : (part + 1) * share_rows, side * columns : (side + 1) * columns
            ] = parted[part, side]


def whole(*operands, parts, turns, capacity, count, identity):
    state_pre, tile_values = operands[-4], operands[-1]
    nodes, columns = state_pre.shape
    blocks, rows, _ = tile_values.shape
    tile_count = nodes // rows
    many = len(turns)
    slots = (parts, capacity, rows, columns)
    dma = pltpu.SemaphoreType.DMA
    return pl.pallas_call(
        functools.partial(
            whole_kernel, count, capacity, 1.0 / math.sqrt(nodes * parts), turns
        ),
        out_shape=(
            jax.ShapeDtypeStruct((nodes, columns), jnp.bfloat16),
            jax.ShapeDtypeStruct((columns, 2 * columns), jnp.float32),
        ),
        in_specs=[smem()] * (len(operands) - 4)
        + [vmem()] * 3
        + [pl.BlockSpec(memory_space=pl.ANY)],
        out_specs=(vmem(), vmem()),
        scratch_shapes=[
            pltpu.VMEM((blocks, rows, rows), jnp.bfloat16),
            pltpu.VMEM((blocks, rows, rows), jnp.bfloat16),
            pltpu.VMEM((tile_count, rows, columns), jnp.bfloat16),
            pltpu.VMEM((tile_count, rows, columns), jnp.float32),
            pltpu.VMEM((2, nodes, columns), jnp.bfloat16),
            pltpu.VMEM((tile_count, rows, columns), jnp.bfloat16),
            pltpu.VMEM((capacity, rows, columns), jnp.bfloat16),
            pltpu.VMEM(slots, jnp.bfloat16),
            pltpu.VMEM(slots, jnp.bfloat16),
            pltpu.VMEM(slots, jnp.bfloat16),
            pltpu.VMEM(slots, jnp.bfloat16),
            pltpu.VMEM(slots, jnp.bfloat16),
            pltpu.VMEM((blocks, rows, columns), jnp.float32),
            pltpu.VMEM((nodes, columns), jnp.bfloat16),
            pltpu.VMEM((2, columns, columns), jnp.float32),
            pltpu.VMEM((parts, 2, columns // parts, columns), jnp.float32),
            pltpu.VMEM((2, columns // parts, columns), jnp.float32),
            pltpu.VMEM((parts, 2, columns // parts, columns), jnp.float32),
            dma,
            dma((ITERS + 1, 4)),
            dma((ITERS + 1, 4)),
            dma((ITERS, many)),
            dma((ITERS, many)),
            dma((many,)),
            dma((many,)),
            dma((many,)),
            dma((many,)),
            dma((many,)),
            dma((many,)),
        ],
        compiler_params=pltpu.CompilerParams(
            collective_id=identity, has_side_effects=True, vmem_limit_bytes=60 * 1024 * 1024
        ),
        name="whole",
    )(*operands)


def swap_kernel(in_ref, out_ref, send_sem, recv_sem):
    other = {"rep": 1 - lax.axis_index("rep")}
    greet([other])
    copy = remote(in_ref, out_ref, send_sem, recv_sem, other)
    copy.start()
    copy.wait()


def swap(array):
    return pl.pallas_call(
        swap_kernel,
        out_shape=jax.ShapeDtypeStruct(array.shape, array.dtype),
        in_specs=[pl.BlockSpec(memory_space=pl.ANY)],
        out_specs=pl.BlockSpec(memory_space=pl.ANY),
        scratch_shapes=[pltpu.SemaphoreType.DMA, pltpu.SemaphoreType.DMA],
        compiler_params=pltpu.CompilerParams(collective_id=1, has_side_effects=True),
        name="swap",
    )(array)


def columns_product(sum_ref, grad_ref):
    nodes = sum_ref.shape[0]
    step = 1024 if nodes % 1024 == 0 else nodes

    def add(t, total):
        at = tile_rows(t, step)
        return total + lax.dot_general(
            sum_ref[at, :], grad_ref[at, :], (((0,), (0,)), ((), ())),
            preferred_element_type=jnp.float32,
        )

    zero = jnp.zeros((sum_ref.shape[1], grad_ref.shape[1]), jnp.float32)
    return lax.fori_loop(0, nodes // step, add, zero)


def shards(state_pre, loss_grad, weight, live_counts, partners, row_tiles, col_tiles, block_tiles):
    node_slots, columns = state_pre.shape
    partitions = lax.axis_size("dom") * lax.axis_size("sub")
    groups = lax.axis_size("groups")
    me = position()
    near = partitions <= 16 and columns % (8 * partitions) == 0
    block_count = row_tiles.shape[1]
    rows = block_tiles.shape[2]
    tile_count = node_slots // rows
    capacity = max(2, 4 * block_count // (3 * partitions))
    slot_total = partitions * capacity

    with jax.named_scope("tables"):
        table = jnp.stack(
            [
                jnp.pad(row, (0, -row.shape[0] % 128))
                for row in (
                    partners[0, :, 0],
                    row_tiles[0],
                    col_tiles[0],
                    jnp.broadcast_to(live_counts, (block_count,)),
                )
            ]
        )
        table = jnp.pad(table, ((0, 4), (0, 0)))
        if near:
            everyone = table_gather(table, groups, partitions)
        else:
            everyone = lax.all_gather(table, PARTS)[None]
        live_everywhere = (everyone[:, :, 3, 0] + rows - 1) // rows
        part_range = jnp.arange(partitions, dtype=jnp.int32)
        if near:
            group = lax.axis_index("groups")
            partner_each = everyone[:, :, 0, :block_count, None] == part_range
            partner_live = jnp.sum(
                jnp.where(partner_each, live_everywhere[:, None, None, :], 0), axis=3
            )
            alive_each = (everyone[:, :, 1, :block_count] < live_everywhere[:, :, None]) & (
                everyone[:, :, 2, :block_count] < partner_live
            )
            col_each = everyone[:, :, 2, :block_count, None] == jnp.arange(tile_count)
            used = jnp.einsum(
                "gpkq,gpkt->gpqt",
                (partner_each & alive_each[..., None]).astype(jnp.bfloat16),
                col_each.astype(jnp.bfloat16),
                preferred_element_type=jnp.float32,
            )
            away = part_range[:, None] != part_range[None, :]
            tiles_used = jnp.sum((used > 0).astype(jnp.int32), axis=3)
            busiest = jnp.max(jnp.where(away[None], tiles_used, 0))
        else:
            group, busiest = 0, capacity
        everyone = lax.dynamic_index_in_dim(everyone, group, 0, keepdims=False)
        live_tiles = lax.dynamic_index_in_dim(live_everywhere, group, 0, keepdims=False)
        partner_all = everyone[:, 0, :block_count]
        row_all = everyone[:, 1, :block_count]
        col_all = everyone[:, 2, :block_count]
        tile_range = jnp.arange(tile_count, dtype=jnp.int32)
        slot_range = jnp.arange(capacity, dtype=jnp.int32)
        mine = (
            (partner_all == me)
            & (row_all < live_tiles[:, None])
            & (col_all < live_tiles[me])
        )
        wants = jnp.any(mine[:, :, None] & (col_all[:, :, None] == tile_range), axis=1)
        want_place = jnp.cumsum(wants.astype(jnp.int32), axis=1) - 1
        hit = wants[:, :, None] & (want_place[:, :, None] == slot_range)
        wanted = jnp.sum(jnp.where(hit, tile_range[None, :, None], 0), axis=1)
        wanted = jnp.where(jnp.any(hit, axis=1), wanted, tile_count).reshape(slot_total)
        partner, row_tile, col_tile = partners[0, :, 0], row_tiles[0], col_tiles[0]
        partner_live = jnp.sum(
            jnp.where(partner[:, None] == part_range, live_tiles[None, :], 0), axis=1
        )
        alive = (row_tile < live_tiles[me]) & (col_tile < partner_live)
        same_partner = (partner[:, None] == partner[None, :]) & alive[None, :]
        same = same_partner & (col_tile[:, None] == col_tile[None, :])
        order = jnp.arange(block_count, dtype=jnp.int32)
        first = alive & ~jnp.any(same & (order[None, :] < order[:, None]), axis=1)
        lower = same_partner & first[None, :] & (col_tile[None, :] < col_tile[:, None])
        place = jnp.sum(lower.astype(jnp.int32), axis=1)
        slots = jnp.where(alive, partner * capacity + place, -1).astype(jnp.int32)
        firsts = first.astype(jnp.int32)

    tile_values = block_tiles[0]
    rep = lax.axis_index("rep")
    halves = [
        lax.dynamic_slice_in_dim(weight, half * columns, columns, 1) for half in (rep, 1 - rep)
    ]
    own_weight = jnp.concatenate(halves, axis=1)
    if near:
        with jax.named_scope("lists"):
            before = order[None, :] < order[:, None]
            after = order[None, :] > order[:, None]
            ahead = same_partner & (
                (col_tile[None, :] < col_tile[:, None])
                | ((col_tile[None, :] == col_tile[:, None]) & before)
            )
            rank = jnp.sum(ahead.astype(jnp.int32), axis=1)
            closing = alive & ~jnp.any(same & after, axis=1)
            slot_range = jnp.arange(slot_total, dtype=jnp.int32)
            ranked = alive[:, None] & ((partner * capacity + rank)[:, None] == slot_range)
            closed = closing[:, None] & (slots[:, None] == slot_range)

            def pick(hits, values, empty=0):
                return jnp.sum(jnp.where(hits, values[:, None] - empty, 0), axis=0) + empty

            same_row = alive[None, :] & (row_tile[:, None] == row_tile[None, :])
            sooner = alive[None, :] & (
                (row_tile[None, :] < row_tile[:, None])
                | ((row_tile[None, :] == row_tile[:, None]) & before)
            )
            row_rank = jnp.sum(sooner.astype(jnp.int32), axis=1)
            row_first = alive & ~jnp.any(same_row & before, axis=1)
            row_last = alive & ~jnp.any(same_row & after, axis=1)
            row_ranked = alive[:, None] & (row_rank[:, None] == order)
            row_closed = row_last[:, None] & (row_tile[:, None] == tile_range)
            lists = (
                live_counts,
                jnp.where(wanted < tile_count, wanted, 0),
                jnp.where(wants, want_place, -1).reshape(partitions * tile_count),
                pick(ranked, order),
                pick(ranked, row_tile),
                pick(ranked, 1 - firsts),
                pick(closed, rank),
                pick(row_ranked, order),
                pick(row_ranked, slots),
                pick(row_ranked, 1 - row_first.astype(jnp.int32)),
                pick(row_closed, row_rank, -1),
            )
        turns = turns_of(lax.axis_size("dom"), lax.axis_size("sub"))
        counts = list(range(max(1, capacity - 4), capacity + 1))
        branches = [
            functools.partial(
                whole,
                parts=partitions,
                turns=turns,
                capacity=capacity,
                count=count,
                identity=3 + i,
            )
            for i, count in enumerate(counts)
        ]
        chosen = jnp.clip(busiest - counts[0], 0, len(counts) - 1)
        return lax.switch(
            chosen, branches, *lists, state_pre, loss_grad, own_weight, tile_values
        )

    slot_shape = jax.ShapeDtypeStruct((slot_total, rows, columns), jnp.bfloat16)
    node_shape = jax.ShapeDtypeStruct((node_slots, columns), jnp.bfloat16)

    request, adjoint = pl.pallas_call(
        request_kernel,
        out_shape=(slot_shape, node_shape),
        in_specs=[smem(), smem(), vmem(), vmem()],
        out_specs=(vmem(), vmem()),
        scratch_shapes=[pltpu.VMEM((tile_count, rows, columns), jnp.bfloat16)],
        compiler_params=params(),
        name="request",
    )(live_counts, wanted, state_pre, loss_grad)
    received = trade_rows(request)
    gathered_sum = pl.pallas_call(
        gather_kernel,
        out_shape=node_shape,
        in_specs=[smem(), smem(), vmem(), vmem()],
        out_specs=vmem(),
        scratch_shapes=[pltpu.VMEM((tile_count, rows, columns), jnp.float32)],
        compiler_params=params(),
        name="gathered",
    )(slots, row_tile, received, tile_values)

    for iteration in range(ITERS):
        other = swap(adjoint)
        outgoing = pl.pallas_call(
            message_kernel,
            out_shape=slot_shape,
            in_specs=[smem(), smem(), smem(), vmem(), vmem(), vmem(), vmem()],
            out_specs=vmem(),
            scratch_shapes=[pltpu.VMEM((node_slots, columns), jnp.bfloat16)],
            compiler_params=params(),
            name="message",
        )(slots, firsts, row_tile, adjoint, other, own_weight, tile_values)
        incoming = trade_rows(outgoing)
        adjoint = pl.pallas_call(
            pull_kernel,
            out_shape=node_shape,
            in_specs=[smem(), smem(), vmem(), vmem(), vmem()],
            out_specs=vmem(),
            scratch_shapes=[pltpu.VMEM((tile_count, rows, columns), jnp.float32)],
            compiler_params=params(),
            name="pull",
        )(live_counts, wanted, incoming, state_pre, loss_grad)

    local_grad = lax.dot_general(
        gathered_sum,
        lax.all_gather(adjoint, "rep", axis=1, tiled=True),
        (((0,), (0,)), ((), ())),
        preferred_element_type=jnp.float32,
    )
    weight_grad = lax.psum(local_grad, PARTS) / math.sqrt(node_slots * partitions)
    return (adjoint, weight_grad)


def solution(mesh):
    return jax.shard_map(
        shards,
        mesh=mesh,
        in_specs=(
            P(("groups", "dom", "sub"), "rep"),
            P(("groups", "dom", "sub"), "rep"),
            P("rep", None),
            P(("groups", "dom", "sub")),
            P(("groups", "dom", "sub"), None, None),
            P(("groups", "dom", "sub"), None),
            P(("groups", "dom", "sub"), None),
            P(("groups", "dom", "sub"), None, None, None),
        ),
        out_specs=(P(("groups", "dom", "sub"), "rep"), P(("groups", "rep"), None)),
        check_vma=False,
    )
```
